128 devices in a mesh: dp: 4 (over z), vocab: 32 (over x, y, core).
Axes of the slice: x: 4, y: 4, z: 4, core: 2. Of those that a mesh axis runs over, the one named last changes fastest.
Arguments:
- hidden: bfloat16 [1152, 16384], P(('dp', 'vocab')), may hold values from -64 to 64
- head: bfloat16 [65536, 16384], P('vocab', 'dp'), may hold values from -1 to 1
- row_scale: float32 [65536], P('vocab'), may hold values from 1 to 8
- live: int32 [4], replicated, may hold values from 1 to 288, 768 in all
- order: int32 [768], replicated, may hold values from 0 to 767, each once
- beam_log_prob: float32 [1152], P('dp'), may hold values from -8 to 8
- token_length: int32 [1152], P('dp'), may hold values from 1 to 63
- div_ids: int32 [768, 16], P('dp'), may hold values from 0 to 65535
Outputs:
- scored: float32 [768, 65536], P('dp', 'vocab')
- slot_log_normalizer: float32 [1152], P('dp')
The draws below stay inside these ranges and needn't reach their ends.
Inputs may be any that keep to these rules, and one draw needn't show every extreme that they name: order is a permutation; entry k numbers a live beam, counting replica by replica; live beam w of a replica sits in its slot (w mod 32) * 9 + floor(w / 32).
All inputs are finite; a program needn't handle non-finite values.
Results may differ from the reference program's by a relative error of at most 0.0003.
Values may be sent and summed in bfloat16 or wider, within the bound.
A program may use at most 128 MiB of HBM per device.

```python
import math
import jax
import jax.numpy as jnp
import numpy as np
from jax import lax

MODEL_WIDTH = 16384
PEN = 16
ROWS = 768
SLOTS = 288
BEAM_SLOT_TOTAL = 1152
SHARDS = 32
SPD = 9
V = 65536
N_DP = 4


def head_row(key, token):
    sub = jax.random.fold_in(jax.random.fold_in(key, 11), token)
    return jax.random.truncated_normal(sub, -6.0, 6.0, (MODEL_WIDTH,), jnp.float32) / jnp.sqrt(jnp.float32(MODEL_WIDTH))


def draw_head(key, part):
    rows = jax.vmap(lambda t: head_row(key, t))(jnp.arange(V))
    return rows.astype(jnp.bfloat16)


def draw_row_scale(key, part):
    key = jax.random.fold_in(key, 2)
    scale = jnp.exp(jax.random.uniform(key, (V,), jnp.float32, 0.0, jnp.log(8.0)))
    return scale


def draw_hidden(key, part):
    key = jax.random.fold_in(key, 1)
    value_entries = jax.random.truncated_normal(key, -6.0, 6.0, (BEAM_SLOT_TOTAL, MODEL_WIDTH), jnp.float32)
    return value_entries.astype(jnp.bfloat16)


def set_ends(drawn, key, least, high):
    longest = drawn.shape.index(max(drawn.shape))
    spots = []
    for shift in (0, 1):
        where = [jax.random.randint(jax.random.fold_in(key, axis), (), 0, length) for axis, length in enumerate(drawn.shape)]
        where[longest] = (where[longest] + shift) % drawn.shape[longest]
        spots.append(tuple(where))
    return drawn.at[spots[0]].set(least).at[spots[1]].set(high)


def shard_levels(rng, shape, split, least, largest):
    gain, own = 1.0, jax.random.fold_in(rng, 6)
    for position, shards_of in split:
        heights = jnp.exp(jax.random.uniform(jax.random.fold_in(own, position), (shards_of,), jnp.float32, least / len(split), largest / len(split)))
        gain = gain * jnp.repeat(heights, shape[position] // shards_of).reshape([-1 if axis == position else 1 for axis in range(len(shape))])
    return gain


def cumulative_ranks(count, slope):
    portions = [(1 << 20) // math.isqrt(rank ** slope) + 1 for rank in range(1, count + 1)]
    scale = 1 + sum(portions) // (1 << 30)
    return np.cumsum(np.array([max(1, weight // scale) for weight in portions]))


def ranked_ids(rng, dims, amount, lean):
    listing = cumulative_ranks(amount, lean)
    lot = jax.random.randint(jax.random.fold_in(rng, 1), dims, 0, int(listing[amount - 1]))
    grade = jnp.searchsorted(jnp.asarray(listing, jnp.int32), lot, side="right")
    return jax.random.permutation(jax.random.fold_in(rng, 2), amount)[grade].astype(jnp.int32)


def length_profile(count, total, most, skew):
    loads = [(1 << 20) // math.isqrt(grade ** skew) + 1 for grade in range(2, count + 1)]
    rest, counts = total - most - (count - 1), [1] * (count - 1)
    while rest > 0:
        candidates = [i for i in range(count - 1) if counts[i] < most]
        whole, budget = sum([loads[i] for i in candidates]), rest
        for i in candidates:
            more = min(most - counts[i], max(1, budget * loads[i] // whole), rest)
            counts[i] = counts[i] + more
            rest = rest - more
    return np.array([most] + counts)


def ragged(key, amount, total, most, slope):
    if amount == 2:
        one = jax.random.randint(key, (), max(1, total - most), min(most, total - 1) + 1)
        return jnp.stack([one, total - one])
    lengths = jnp.asarray(length_profile(amount, total, most, slope), jnp.int32)
    couples = (amount - 1) // 2
    source_of, receiver = lengths[1:1 + 2 * couples:2], lengths[2:2 + 2 * couples:2]
    room = jnp.minimum(source_of - 1, most - receiver)
    moved = jax.random.randint(jax.random.fold_in(key, 1), (couples,), 0, 1 << 20) % (room + 1)
    lengths = lengths.at[1:1 + 2 * couples:2].set(source_of - moved).at[2:2 + 2 * couples:2].set(receiver + moved)
    return lengths[jax.random.permutation(jax.random.fold_in(key, 2), amount)]


def bell_draw(own_key, shape, spread, limit, split=(), kind=jnp.bfloat16):
    array = spread * jax.random.normal(own_key, shape, jnp.float32)
    if split:
        array = array * shard_levels(own_key, shape, split, -0.22, 0.18)
    return jnp.clip(array, -limit, limit).astype(kind)


def setup_inputs(seed: int = 0) -> dict:
    arg_keys = jax.random.split(jax.random.key(seed), 9)
    return {
        "hidden": draw_hidden(jax.random.fold_in(arg_keys[8], 71), 0),
        "head": draw_head(jax.random.fold_in(arg_keys[8], 71), 0),
        "row_scale": draw_row_scale(jax.random.fold_in(arg_keys[8], 71), 0),
        "live": ragged(arg_keys[3], N_DP, ROWS, SLOTS, 2).astype(jnp.int32),
        "order": jax.random.permutation(arg_keys[4], ROWS).astype(jnp.int32),
        "beam_log_prob": bell_draw(arg_keys[5], (BEAM_SLOT_TOTAL,), 2.0, 8.0, ((0, 4),), jnp.float32),
        "token_length": set_ends(jax.random.randint(arg_keys[6], (BEAM_SLOT_TOTAL,), 1, 64), jax.random.fold_in(arg_keys[6], 1), 1, 63).astype(jnp.int32),
        "div_ids": set_ends(ranked_ids(arg_keys[7], (ROWS, PEN), V, 2), jax.random.fold_in(arg_keys[7], 3), 0, V - 1).astype(jnp.int32),
    }


def reference(hidden, head, row_scale, live, order, beam_log_prob, token_length, div_ids):
    ends = jnp.cumsum(live).astype(jnp.int32)
    starts = (ends - live).astype(jnp.int32)
    replica = jnp.sum((order[:, None] >= ends[None, :]).astype(jnp.int32), axis=1).astype(jnp.int32)
    within = (order - starts[replica]).astype(jnp.int32)
    slot_position = (replica * SLOTS + (within % SHARDS) * SPD + within // SHARDS).astype(jnp.int32)
    picked = hidden[slot_position]
    logits = lax.dot_general(picked, head, (((1,), (1,)), ((), ())), preferred_element_type=jnp.float32)
    logits = logits * row_scale[None, :]
    top = jnp.max(logits, axis=1)
    log_sum_exponent = top + jnp.log(jnp.sum(jnp.exp(logits - top[:, None]), axis=1))
    length_factor = ((5.0 + token_length.astype(jnp.float32)) / 6.0) ** 0.8
    count = jnp.zeros((ROWS, V), jnp.float32).at[jnp.arange(ROWS)[:, None], div_ids].add(1.0)
    scored = (beam_log_prob[slot_position][:, None] + logits - log_sum_exponent[:, None] - 0.5 * count) / length_factor[slot_position][:, None]
    slot_log_normalizer = jnp.zeros((BEAM_SLOT_TOTAL,), jnp.float32).at[slot_position].set(log_sum_exponent)
    return scored, slot_log_normalizer
```

```python
import functools

import jax
import jax.numpy as jnp
from jax import lax
from jax.experimental import pallas as pl
from jax.experimental.pallas import tpu as pltpu
from jax.sharding import PartitionSpec as P

F32, BF16, I32, I16 = jnp.float32, jnp.bfloat16, jnp.int32, jnp.int16
MESH = pl.DeviceIdType.MESH

STEPS_ANY = ((4, 0, 48), (4, 48, 96), (4, 96, 144), (4, 144, 192))
CAP = 32
RB = 16


def iota(shape, axis):
    return lax.broadcasted_iota(I32, shape, axis)


def to_col(row, n, shift=0):
    width = row.shape[1]
    hit = iota((n, width), 0) + shift == iota((n, width), 1)
    return jnp.sum(jnp.where(hit, row, jnp.zeros_like(row)), axis=1, keepdims=True)


def to_row(col, width, shift=0):
    n = col.shape[0]
    hit = iota((n, width), 0) + shift == iota((n, width), 1)
    return jnp.sum(jnp.where(hit, col, jnp.zeros_like(col)), axis=0, keepdims=True)


def live_of_lane(count, lane):
    return (count - lane + 31) >> 5


def row_info(order, live):
    e0 = live[0]
    e1 = e0 + live[1]
    e2 = e1 + live[2]
    past = [(order >= e).astype(I32) for e in (e0, e1, e2)]
    replica = past[0] + past[1] + past[2]
    within = order - (past[0] * live[0] + past[1] * live[1] + past[2] * live[2])
    lane, depth = within & 31, within >> 5
    row = depth
    for i in range(3):
        row = row + past[i] * live_of_lane(live[i], lane)
    return replica, lane, depth, row


def place(lane, x, y):
    lx, ly, lc = lane >> 3, (lane >> 1) & 3, lane & 1
    dx, dy = (lx - x) & 3, (ly - y) & 3
    r1 = dx + lc * (dy - dx)
    r2 = dy + lc * (dx - dy)
    g1, g2 = r1 ^ (r1 >> 1), r2 ^ (r2 >> 1)
    near = (g2 == 1) | (g2 == 2)
    chunk = jnp.where(g2 == 0, 0, jnp.where(g2 == 3, 3, 1 + (g1 >> 1)))
    minor = jnp.where(near, (g2 - 1) * 2 + (g1 & 1), g1)
    return chunk, chunk * 8 + lc * 4 + minor


def quantize(val):
    top = jnp.maximum(jnp.max(jnp.abs(val), axis=1, keepdims=True), 1e-30)
    coded = jnp.round(val * (32767.0 / top)).astype(I32).astype(I16)
    return coded, top * (1.0 / 32767.0)


def widen(coded):
    return coded.astype(I32).astype(F32)


def kernel(steps, by_arrival,
           hidden, head, row_scale, live, order, blp, tlen, div,
           scored, slotn,
           hrecv, pool, headv, st, pos, sel, xsel, S,
           SP, SM, RM, RP, SP2, SM2, RM2, RP2,
           CP, CM, KM, KP, CP2, CM2, KM2, KP2,
           TA, TB, LS,
           head_sem, own_sem, z_s, z_r, t_s, t_r,
           r1_s, r1_r, r2_s, r2_r, sib_s, sib_r,
           rs_s, rs_r, ta_s, ta_r, tb_s, tb_r, ls_s, ls_r):
    q = lax.axis_index("dp")
    v = lax.axis_index("vocab")
    x, y, c = v // 8, (v // 2) % 4, v % 2
    width = hidden.shape[1] // 4
    half_v = head.shape[0] // 2
    voc = head.shape[0]
    rows_g = order.shape[1]
    slots = blp.shape[1]
    n_steps = len(steps)

    def dev(zz, xx, yy, cc):
        return (zz % 4, (xx % 4) * 8 + (yy % 4) * 2 + (cc % 2))

    zdev = [dev(q + d, x, y, c) for d in range(4)]
    fan = [(dy, dc) for dy in range(4) for dc in range(2)]
    adev = [dev(q, x, y + dy, c + dc) for dy, dc in fan]
    bdev = [dev(q, x + d, y, c) for d in range(4)]
    sibling = adev[1]
    r1p = dev(q, x + (1 - c), y + c, c)
    r1m = dev(q, x + 3 * (1 - c), y + 3 * c, c)
    r2p = dev(q, x + c, y + (1 - c), c)
    r2m = dev(q, x + 3 * c, y + 3 * (1 - c), c)
    sends = []

    def rc(src, dst, ss, rs, device):
        return pltpu.make_async_remote_copy(
            src_ref=src, dst_ref=dst, send_sem=ss, recv_sem=rs, device_id=device, device_id_type=MESH)

    def push(src, dst, ss, rs, device):
        copy = rc(src, dst, ss, rs, device)
        copy.start()
        sends.append(copy)

    def got(dst, rs):
        rc(dst, dst, z_s.at[0], rs, zdev[1]).wait_recv()

    head_copy = pltpu.make_async_copy(head, headv, head_sem)
    head_copy.start()
    own_copy = pltpu.make_async_copy(
        hidden.at[:, pl.ds(pl.multiple_of(q * width, width), width)], hrecv.at[q], own_sem)
    own_copy.start()
    st[q] = jnp.zeros(st.shape[1:], F32)
    st[q, 0:1, 0:slots] = blp[...]
    st[q, 1:2, 0:slots] = jnp.exp(0.8 * jnp.log((5.0 + tlen[...].astype(F32)) / 6.0))
    for ref in (CP, CM, CP2, CM2):
        ref[...] = jnp.zeros(ref.shape, F32)
    TA[0] = jnp.zeros(TA.shape[1:], F32)
    TB[0] = jnp.zeros(TB.shape[1:], F32)
    LS[q] = jnp.zeros(LS.shape[1:], F32)

    barrier = pltpu.get_barrier_semaphore()
    peers = zdev[1:] + adev[1:] + bdev[1:]
    for device in peers:
        pl.semaphore_signal(barrier, inc=1, device_id=device, device_id_type=MESH)
    pl.semaphore_wait(barrier, len(peers))

    for d in (2, 1, 3):
        to = (q + d) % 4
        push(hidden.at[:, pl.ds(pl.multiple_of(to * width, width), width)], hrecv.at[q],
             z_s.at[d - 1], z_r.at[d - 1], zdev[d])
    for d in (1, 2, 3):
        push(st.at[q], st.at[q], t_s.at[d - 1], t_r.at[d - 1], zdev[d])

    groups = [(q + 2) % 4, (q + 1) % 4, (q + 3) % 4, q]
    own_rank = None
    for gi in range(4):
        o = order[pl.ds(groups[gi], 1), :]
        replica, lane, depth, row = row_info(o, live)
        chunk, block = place(lane, x, y)
        where_row = block * CAP + row
        if by_arrival:
            key = chunk * 256 + iota((1, rows_g), 1)
            rank = jnp.sum((to_col(key, rows_g) < key).astype(I32), axis=0, keepdims=True)
        else:
            rank = iota((1, rows_g), 1)
        hit = iota((rows_g, rows_g), 0) == rank
        col = jnp.sum(jnp.where(hit, where_row, 0), axis=1, keepdims=True)
        pos[gi * rows_g:(gi + 1) * rows_g, :] = jnp.broadcast_to(col, (rows_g, 128))
        own_rank = rank

    own_copy.wait()
    for d in (1, 3, 2):
        got(hrecv.at[(q + 4 - d) % 4], z_r.at[d - 1])
    counts = [live_of_lane(live[r], v) for r in range(4)]
    picks = []
    first = 0
    for r in range(4):
        i, j = iota((CAP, 9), 0), iota((CAP, 9), 1)
        picks.append(jnp.where((i == first + j) & (j < counts[r]), 1.0, 0.0).astype(BF16))
        first = first + counts[r]

    def blk(idx):
        return pool.at[pl.ds(pl.multiple_of(idx * CAP, CAP), CAP), :]

    def half(idx, h):
        return pool.at[pl.ds(pl.multiple_of(idx * CAP + h * (CAP // 2), CAP // 2), CAP // 2), :]

    t4 = 4 * c
    u4 = 4 - t4
    span = 1024
    for k in range(width // span):
        cols = slice(k * span, (k + 1) * span)
        acc = jnp.zeros((CAP, span), F32)
        for r in range(4):
            acc += jnp.dot(picks[r], hrecv[r, :, cols], preferred_element_type=F32)
        pool[pl.ds(pl.multiple_of(t4 * CAP, CAP), CAP), cols] = acc.astype(BF16)

    def to_sibling(ch, m):
        push(blk(ch * 8 + t4 + m), blk(ch * 8 + t4 + m), sib_s.at[ch * 4 + m], sib_r.at[ch * 4 + m], sibling)

    def from_sibling(ch):
        for m in range(4):
            got(blk(ch * 8 + u4 + m), sib_r.at[ch * 4 + m])

    def spread(m):
        ch, mm = 1 + (m >> 1), m & 1
        push(blk(t4 + m), blk(ch * 8 + t4 + 2 + mm), r2_s.at[2 * m + 1], r2_r.at[2 * m + 1], r2p)
        push(blk(t4 + m), blk(ch * 8 + t4 + mm), r2_s.at[2 * m], r2_r.at[2 * m], r2m)

    def gather_chunk(ch):
        if ch == 0:
            push(blk(t4), blk(t4 + 2), r1_s.at[1], r1_r.at[1], r1p)
            push(blk(t4), blk(t4 + 1), r1_s.at[0], r1_r.at[0], r1m)
            to_sibling(0, 0)
            spread(0)
            got(blk(t4 + 1), r1_r.at[0])
            push(half(t4 + 1, 0), half(t4 + 3, 0), r1_s.at[2], r1_r.at[2], r1m)
            got(blk(t4 + 2), r1_r.at[1])
            push(half(t4 + 2, 1), half(t4 + 3, 1), r1_s.at[3], r1_r.at[3], r1p)
            to_sibling(0, 1)
            to_sibling(0, 2)
            spread(1)
            spread(2)
            got(half(t4 + 3, 0), r1_r.at[2])
            got(half(t4 + 3, 1), r1_r.at[3])
            to_sibling(0, 3)
            spread(3)
        elif ch < 3:
            for mm in range(2):
                m = 2 * (ch - 1) + mm
                got(blk(ch * 8 + t4 + mm), r2_r.at[2 * m])
                push(half(ch * 8 + t4 + mm, 0), half(24 + t4 + m, 0), r2_s.at[8 + 2 * m], r2_r.at[8 + 2 * m], r2m)
                to_sibling(ch, mm)
                got(blk(ch * 8 + t4 + 2 + mm), r2_r.at[2 * m + 1])
                push(half(ch * 8 + t4 + 2 + mm, 1), half(24 + t4 + m, 1),
                     r2_s.at[9 + 2 * m], r2_r.at[9 + 2 * m], r2p)
                to_sibling(ch, 2 + mm)
        else:
            for m in range(4):
                got(half(24 + t4 + m, 0), r2_r.at[8 + 2 * m])
                got(half(24 + t4 + m, 1), r2_r.at[9 + 2 * m])
                to_sibling(3, m)
        from_sibling(ch)

    def multiply(s):
        n_ch, lo, hi = steps[s]
        m = hi - lo
        wide = n_ch * 8 * CAP
        for gi in range(4):
            at = pos[gi * rows_g + lo:gi * rows_g + hi, :]
            for b in range(wide // 128):
                hit = at == iota((m, 128), 1) + 128 * b
                sel[gi * m:(gi + 1) * m, b * 128:(b + 1) * 128] = jnp.where(hit, 1.0, 0.0).astype(BF16)

        @pl.loop(0, width // 512)
        def _(n):
            cols = pl.ds(pl.multiple_of(n * 512, 512), 512)
            xsel[0:4 * m, cols] = jnp.dot(
                sel[0:4 * m, 0:wide], pool[0:wide, cols], preferred_element_type=F32).astype(BF16)

        if s == 0:
            head_copy.wait()

        @pl.loop(0, voc // 256)
        def _(n):
            cols = pl.ds(pl.multiple_of(n * 256, 256), 256)
            out = lax.dot_general(xsel[0:4 * m, :], headv[cols, :], (((1,), (1,)), ((), ())),
                                  preferred_element_type=F32)
            for gi in range(4):
                S[gi * rows_g + lo:gi * rows_g + hi, cols] = out[gi * m:(gi + 1) * m, :]

    def blocks(s, body):
        _, lo, hi = steps[s]

        @pl.loop(0, (hi - lo) // RB)
        def _(b):
            shift = pl.multiple_of(b * RB, RB)
            body(shift, pl.multiple_of(lo + shift, RB))

    H0, H1 = slice(0, half_v), slice(half_v, 2 * half_v)

    def rows_of(gi, rows):
        return pl.ds(pl.multiple_of(gi * rows_g + rows, RB), RB)

    def send_first(s):
        _, lo, hi = steps[s]

        def body(shift, rows):
            r = pl.ds(rows, RB)
            for buf, scales, line, gi, src, dst in (
                    (SP, CP, 0, 0, H0, H0), (SM, CM, 1, 0, H1, H1),
                    (SP, CP, 1, 1, H1, H1), (SM, CM, 0, 2, H0, H0)):
                coded, scale = quantize(S[rows_of(gi, rows), src])
                buf[r, dst] = coded
                scales[s, line:line + 1, :] += to_row(scale, 128, shift)

        blocks(s, body)
        push(SP.at[lo:hi, :], RM.at[lo:hi, :], rs_s.at[s, 0], rs_r.at[s, 0], zdev[1])
        push(SM.at[lo:hi, :], RP.at[lo:hi, :], rs_s.at[s, 1], rs_r.at[s, 1], zdev[3])
        push(CP.at[s], KM.at[s], rs_s.at[s, 2], rs_r.at[s, 2], zdev[1])
        push(CM.at[s], KP.at[s], rs_s.at[s, 3], rs_r.at[s, 3], zdev[3])

    def send_second(s):
        _, lo, hi = steps[s]
        got(RM.at[lo:hi, :], rs_r.at[s, 0])
        got(RP.at[lo:hi, :], rs_r.at[s, 1])
        got(KM.at[s], rs_r.at[s, 2])
        got(KP.at[s], rs_r.at[s, 3])

        def body(shift, rows):
            r = pl.ds(rows, RB)
            for buf, scales, recv, rscale, line, gi, cols in (
                    (SP2, CP2, RM, KM, 0, 1, H0), (SM2, CM2, RP, KP, 1, 2, H1)):
                old = widen(recv[r, cols]) * to_col(rscale[s, line:line + 1, :], RB, shift)
                coded, scale = quantize(S[rows_of(gi, rows), cols] + old)
                buf[r, :] = coded
                scales[s, 0:1, :] += to_row(scale, 128, shift)

        blocks(s, body)
        push(SP2.at[lo:hi, :], RM2.at[lo:hi, :], rs_s.at[s, 4], rs_r.at[s, 4], zdev[1])
        push(SM2.at[lo:hi, :], RP2.at[lo:hi, :], rs_s.at[s, 5], rs_r.at[s, 5], zdev[3])
        push(CP2.at[s], KM2.at[s], rs_s.at[s, 6], rs_r.at[s, 6], zdev[1])
        push(CM2.at[s], KP2.at[s], rs_s.at[s, 7], rs_r.at[s, 7], zdev[3])

    def finish(s):
        _, lo, hi = steps[s]
        got(RM2.at[lo:hi, :], rs_r.at[s, 4])
        got(RP2.at[lo:hi, :], rs_r.at[s, 5])
        got(KM2.at[s], rs_r.at[s, 6])
        got(KP2.at[s], rs_r.at[s, 7])

        def body(shift, rows):
            r = pl.ds(rows, RB)
            mine = rows_of(3, rows)

            def col(ref, line):
                return to_col(ref[s, line:line + 1, :], RB, shift)

            l0 = (S[mine, H0] + widen(RM2[r, :]) * col(KM2, 0) + widen(RP[r, H0]) * col(KP, 0)) * row_scale[:, H0]
            l1 = (S[mine, H1] + widen(RP2[r, :]) * col(KP2, 0) + widen(RM[r, H1]) * col(KM, 1)) * row_scale[:, H1]
            S[mine, H0] = l0
            S[mine, H1] = l1
            top = jnp.maximum(jnp.max(l0, axis=1, keepdims=True), jnp.max(l1, axis=1, keepdims=True))
            total = jnp.sum(jnp.exp(l0 - top), axis=1, keepdims=True) + jnp.sum(jnp.exp(l1 - top), axis=1, keepdims=True)
            TA[0, 0:1, :] += to_row(top, 256, rows)
            TA[0, 1:2, :] += to_row(total, 256, rows)

        blocks(s, body)

    done_ch = 0
    for s in range(n_steps):
        while done_ch < steps[s][0]:
            gather_chunk(done_ch)
            done_ch += 1
        multiply(s)
        send_first(s)
        if s >= 1:
            send_second(s - 1)
        if s >= 2:
            finish(s - 2)

    base = v * voc

    @pl.loop(0, rows_g // RB)
    def _(b):
        r = pl.ds(pl.multiple_of(b * RB, RB), RB)
        ids = div[r, :] - base
        for k in range(voc // 512):
            token = iota((RB, 512), 1) + k * 512
            acc = jnp.zeros((RB, 512), F32)
            for j in range(16):
                acc = acc - jnp.where(ids[:, j:j + 1] == token, 0.5, 0.0)
            scored[r, k * 512:(k + 1) * 512] = acc

    send_second(n_steps - 1)

    for d in (1, 2, 3):
        got(st.at[(q + 4 - d) % 4], t_r.at[d - 1])
    replica, lane, depth, _ = row_info(order[pl.ds(q, 1), :], live)
    slot_col = to_col(replica * slots + lane * 9 + depth, rows_g)
    rank_col = to_col(own_rank, rows_g)
    score = jnp.zeros((rows_g, 1), F32)
    factor = jnp.zeros((rows_g, 1), F32)
    for r in range(4):
        hit = slot_col - r * slots == iota((rows_g, st.shape[2]), 1)
        score += jnp.sum(jnp.where(hit, st[r, 0:1, :], 0.0), axis=1, keepdims=True)
        factor += jnp.sum(jnp.where(hit, st[r, 1:2, :], 0.0), axis=1, keepdims=True)
    inverse = 1.0 / factor
    perm = rank_col == iota((rows_g, 256), 1)
    permute = jnp.where(rank_col == iota((rows_g, rows_g), 1), 1.0, 0.0)

    if n_steps >= 2:
        finish(n_steps - 2)
    finish(n_steps - 1)

    for i in range(1, 8):
        push(TA.at[0], TA.at[i], ta_s.at[i], ta_r.at[i], adev[i])

    @pl.loop(0, voc // 256)
    def _(n):
        cols = pl.ds(pl.multiple_of(n * 256, 256), 256)
        scored[:, cols] += jnp.dot(permute, S[3 * rows_g:4 * rows_g, cols], precision=lax.Precision.HIGHEST,
                                   preferred_element_type=F32)

    def combine(ref, n):
        tops = [ref[i, 0:1, :] for i in range(n)]
        top = functools.reduce(jnp.maximum, tops)
        total = sum(ref[i, 1:2, :] * jnp.exp(tops[i] - top) for i in range(n))
        return top, total

    for i in range(1, 8):
        got(TA.at[i], ta_r.at[i])
    top, total = combine(TA, 8)
    TB[0, 0:1, :] = top
    TB[0, 1:2, :] = total
    for i in range(1, 4):
        push(TB.at[0], TB.at[i], tb_s.at[i], tb_r.at[i], bdev[i])
    for i in range(1, 4):
        got(TB.at[i], tb_r.at[i])
    top, total = combine(TB, 4)
    lse_rank = top + jnp.log(total)
    lse = jnp.sum(jnp.where(perm, lse_rank, 0.0), axis=1, keepdims=True)
    LS[q, 0:1, :] = to_row(lse, 256)
    for d in (1, 2, 3):
        push(LS.at[q], LS.at[q], ls_s.at[d - 1], ls_r.at[d - 1], zdev[d])
    shift_col = score - lse
    for k in range(voc // 256):
        cols = slice(k * 256, (k + 1) * 256)
        scored[:, cols] = (scored[:, cols] + shift_col) * inverse

    for d in (1, 2, 3):
        got(LS.at[(q + 4 - d) % 4], ls_r.at[d - 1])
    acc = jnp.zeros((1, st.shape[2]), F32)
    for g in range(4):
        replica, lane, depth, _ = row_info(order[g:g + 1, :], live)
        slot_col = to_col(replica * slots + lane * 9 + depth, rows_g)
        lse_col = to_col(LS[g, 0:1, :], rows_g)
        hit = slot_col - q * slots == iota((rows_g, st.shape[2]), 1)
        acc += jnp.sum(jnp.where(hit, lse_col, 0.0), axis=0, keepdims=True)
    slotn[...] = acc[:, 0:slots]

    for copy in sends:
        copy.wait_send()


def call(steps, by_arrival, ident, hidden, head, row_scale, live, order, blp, tlen, div):
    rows_g, voc, width, slots = order.shape[1], head.shape[0], head.shape[1], blp.shape[1]
    half_v = voc // 2
    n = len(steps)
    tall = 4 * max(hi - lo for _, lo, hi in steps)
    dma = pltpu.SemaphoreType.DMA
    vmem = pl.BlockSpec(memory_space=pltpu.VMEM)
    anyspace = pl.BlockSpec(memory_space=pl.ANY)
    smem = pl.BlockSpec(memory_space=pltpu.SMEM)
    return pl.pallas_call(
        functools.partial(kernel, steps, by_arrival),
        out_shape=(jax.ShapeDtypeStruct((rows_g, voc), F32), jax.ShapeDtypeStruct((1, slots), F32)),
        in_specs=[anyspace, anyspace, vmem, smem, vmem, vmem, vmem, vmem],
        out_specs=(vmem, vmem),
        scratch_shapes=[
            pltpu.VMEM((4, hidden.shape[0], width), BF16),
            pltpu.VMEM((32 * CAP, width), BF16),
            pltpu.VMEM((voc, width), BF16),
            pltpu.VMEM((4, 8, 384), F32),
            pltpu.VMEM((4 * rows_g, 128), I32),
            pltpu.VMEM((tall, 32 * CAP), BF16),
            pltpu.VMEM((tall, width), BF16),
            pltpu.VMEM((4 * rows_g, voc), F32),
            *[pltpu.VMEM((rows_g, voc), I16)] * 4,
            *[pltpu.VMEM((rows_g, half_v), I16)] * 4,
            *[pltpu.VMEM((n, 8, 128), F32)] * 8,
            pltpu.VMEM((8, 8, 256), F32),
            pltpu.VMEM((4, 8, 256), F32),
            pltpu.VMEM((4, 8, 256), F32),
            dma, dma,
            dma((3,)), dma((3,)), dma((3,)), dma((3,)),
            dma((4,)), dma((4,)), dma((16,)), dma((16,)), dma((16,)), dma((16,)),
            dma((n, 8)), dma((n, 8)), dma((8,)), dma((8,)), dma((4,)), dma((4,)), dma((3,)), dma((3,)),
        ],
        compiler_params=pltpu.CompilerParams(
            collective_id=ident, has_side_effects=True, vmem_limit_bytes=60 * 1024 * 1024),
    )(hidden, head, row_scale, live, order, blp, tlen, div)


def per_device(hidden, head, row_scale, live, order, beam_log_prob, token_length, div_ids):
    groups = lax.axis_size("dp")
    scored, slot = call(
        STEPS_ANY, False, 0, hidden, head, row_scale[None, :], live, order.reshape(groups, -1),
        beam_log_prob[None, :], token_length[None, :], div_ids)
    return scored, slot[0]


def solution(mesh):
    return jax.shard_map(
        per_device,
        mesh=mesh,
        in_specs=(
            P(("dp", "vocab"), None),
            P("vocab", "dp"),
            P("vocab"),
            P(),
            P(),
            P("dp"),
            P("dp"),
            P("dp", None),
        ),
        out_specs=(P("dp", "vocab"), P("dp")),
        check_vma=False,
    )
```

```python
import functools

import jax
import jax.numpy as jnp
from jax import lax
from jax.experimental import pallas as pl
from jax.experimental.pallas import tpu as pltpu
from jax.sharding import PartitionSpec as P

F32, BF16, I32, I16 = jnp.float32, jnp.bfloat16, jnp.int32, jnp.int16
MESH = pl.DeviceIdType.MESH

PARTS = ((0, 1024), (1024, 1024), (2048, 1024), (3072, 512), (3584, 512))
CAP = 32
RB = 64
PIECE = 512


def iota(shape, axis):
    return lax.broadcasted_iota(I32, shape, axis)


def to_col(row, n, shift=0):
    width = row.shape[1]
    hit = iota((n, width), 0) + shift == iota((n, width), 1)
    return jnp.sum(jnp.where(hit, row, jnp.zeros_like(row)), axis=1, keepdims=True)


def to_row(col, width, shift=0):
    n = col.shape[0]
    hit = iota((n, width), 0) + shift == iota((n, width), 1)
    return jnp.sum(jnp.where(hit, col, jnp.zeros_like(col)), axis=0, keepdims=True)


def live_of_lane(count, lane):
    return (count - lane + 31) >> 5


def row_info(order, live):
    e0 = live[0]
    e1 = e0 + live[1]
    e2 = e1 + live[2]
    past = [(order >= e).astype(I32) for e in (e0, e1, e2)]
    replica = past[0] + past[1] + past[2]
    within = order - (past[0] * live[0] + past[1] * live[1] + past[2] * live[2])
    lane, depth = within & 31, within >> 5
    row = depth
    for i in range(3):
        row = row + past[i] * live_of_lane(live[i], lane)
    return replica, lane, depth, row


def place(lane, x, y):
    lx, ly, lc = lane >> 3, (lane >> 1) & 3, lane & 1
    dx, dy = (lx - x) & 3, (ly - y) & 3
    r1 = dx + lc * (dy - dx)
    r2 = dy + lc * (dx - dy)
    return (r2 ^ (r2 >> 1)) * 8 + lc * 4 + (r1 ^ (r1 >> 1))


def quantize(val):
    top = jnp.maximum(jnp.max(jnp.abs(val), axis=1, keepdims=True), 1e-30)
    coded = jnp.round(val * (32767.0 / top)).astype(I32).astype(I16)
    return coded, top * (1.0 / 32767.0)


def widen(coded):
    return coded.astype(I32).astype(F32)


def kernel(hidden, head, row_scale, live, order, blp, tlen, div,
           scored, slotn,
           hrecv, pool, headv, st, sel, xsel, S, CN,
           SP, SM, RM, RP, SP2, SM2, RM2, RP2,
           CP, CM, KM, KP, CP2, CM2, KM2, KP2,
           TA, TB, LS,
           head_sem, own_sem, out_sem, z_s, z_r, t_s, t_r,
           r1_s, r1_r, r2_s, r2_r, sib_s, sib_r,
           rs_s, rs_r, rt_s, rt_r, ta_s, ta_r, tb_s, tb_r, ls_s, ls_r):
    q = lax.axis_index("dp")
    v = lax.axis_index("vocab")
    x, y, c = v // 8, (v // 2) % 4, v % 2
    width = hidden.shape[1] // 4
    voc = head.shape[0]
    half_v = voc // 2
    rows_g = div.shape[1]
    slots = blp.shape[0]
    n_parts = len(PARTS)

    def dev(zz, xx, yy, cc):
        return (zz % 4, (xx % 4) * 8 + (yy % 4) * 2 + (cc % 2))

    zdev = [dev(q + d, x, y, c) for d in range(4)]
    fan = [(dy, dc) for dy in range(4) for dc in range(2)]
    adev = [dev(q, x, y + dy, c + dc) for dy, dc in fan]
    bdev = [dev(q, x + d, y, c) for d in range(4)]
    sibling = adev[1]
    r1p = dev(q, x + (1 - c), y + c, c)
    r1m = dev(q, x + 3 * (1 - c), y + 3 * c, c)
    r2p = dev(q, x + c, y + (1 - c), c)
    r2m = dev(q, x + 3 * c, y + 3 * (1 - c), c)
    sends = []

    def rc(src, dst, ss, rs, device):
        return pltpu.make_async_remote_copy(
            src_ref=src, dst_ref=dst, send_sem=ss, recv_sem=rs, device_id=device, device_id_type=MESH)

    def push(src, dst, ss, rs, device):
        copy = rc(src, dst, ss, rs, device)
        copy.start()
        sends.append(copy)

    def got(dst, rs):
        rc(dst, dst, t_s.at[0], rs, zdev[1]).wait_recv()

    barrier = pltpu.get_barrier_semaphore()
    peers = zdev[1:] + adev[1:] + bdev[1:]
    for device in peers:
        pl.semaphore_signal(barrier, inc=1, device_id=device, device_id_type=MESH)

    def part(k):
        return pl.ds(PARTS[k][0], PARTS[k][1])

    def quarter(group, k):
        at = pl.multiple_of(group * width + PARTS[k][0], 128)
        return hidden.at[:, pl.ds(at, PARTS[k][1])]

    own_copies = [pltpu.make_async_copy(quarter(q, k), hrecv.at[q, :, part(k)], own_sem.at[k]) for k in range(n_parts)]
    head_copies = [pltpu.make_async_copy(head.at[:, part(k)], headv.at[:, part(k)], head_sem.at[k])
                   for k in range(n_parts)]
    for copy in own_copies + head_copies:
        copy.start()
    st[q] = jnp.zeros(st.shape[1:], F32)
    st[q, 0:1, 0:slots] = blp[...].reshape(1, slots)
    lengths = tlen[...].reshape(1, slots).astype(F32)
    st[q, 1:2, 0:slots] = jnp.exp(0.8 * jnp.log((5.0 + lengths) / 6.0))
    for ref in (CP, CM, CP2, CM2):
        ref[...] = jnp.zeros(ref.shape, F32)
    TA[0] = jnp.zeros(TA.shape[1:], F32)
    TB[0] = jnp.zeros(TB.shape[1:], F32)
    LS[q] = jnp.zeros(LS.shape[1:], F32)

    pl.semaphore_wait(barrier, len(peers))

    for k in range(n_parts):
        for d in (2, 1, 3):
            push(quarter((q + d) % 4, k), hrecv.at[q, :, part(k)], z_s.at[k, d - 1], z_r.at[k, d - 1], zdev[d])
    for d in (1, 2, 3):
        push(st.at[q], st.at[q], t_s.at[d - 1], t_r.at[d - 1], zdev[d])

    numbers = order[...].reshape(1, 4 * rows_g)
    by_group = [numbers[:, g * rows_g:(g + 1) * rows_g] for g in range(4)]

    def order_of(group):
        return sum(jnp.where(group == g, by_group[g], 0) for g in range(4))

    for gi, group in enumerate(((q + 2) % 4, (q + 1) % 4, (q + 3) % 4, q)):
        _, lane, _, row = row_info(order_of(group), live)
        at = to_col(place(lane, x, y) * CAP + row, rows_g)
        for b in range(32 * CAP // 128):
            hit = at == iota((rows_g, 128), 1) + 128 * b
            sel[gi * rows_g:(gi + 1) * rows_g, b * 128:(b + 1) * 128] = jnp.where(hit, 1.0, 0.0).astype(BF16)

    counts = [live_of_lane(live[r], v) for r in range(4)]
    picks = []
    first = 0
    for r in range(4):
        i, j = iota((CAP, 9), 0), iota((CAP, 9), 1)
        picks.append(jnp.where((i == first + j) & (j < counts[r]), 1.0, 0.0).astype(BF16))
        first = first + counts[r]

    t4 = 4 * c
    u4 = 4 - t4

    def blk(idx, k, n=1):
        return pool.at[pl.ds(pl.multiple_of(idx * CAP, CAP), n * CAP), part(k)]

    def half(idx, h, k):
        return pool.at[pl.ds(pl.multiple_of(idx * CAP + h * (CAP // 2), CAP // 2), CAP // 2), part(k)]

    def to_sibling(r2, k):
        push(blk(r2 * 8 + t4, k, 4), blk(r2 * 8 + t4, k, 4), sib_s.at[k, r2], sib_r.at[k, r2], sibling)

    def stage1(k):
        own_copies[k].wait()
        for d in (1, 3, 2):
            got(hrecv.at[(q + 4 - d) % 4, :, part(k)], z_r.at[k, d - 1])
        acc = jnp.zeros((CAP, PARTS[k][1]), F32)
        for r in range(4):
            acc += jnp.dot(picks[r], hrecv[r, :, part(k)], preferred_element_type=F32)
        pool[pl.ds(pl.multiple_of(t4 * CAP, CAP), CAP), part(k)] = acc.astype(BF16)
        push(blk(t4, k), blk(t4 + 2, k), r1_s.at[k, 1], r1_r.at[k, 1], r1p)
        push(blk(t4, k), blk(t4 + 1, k), r1_s.at[k, 0], r1_r.at[k, 0], r1m)

    def stage2(k):
        got(blk(t4 + 1, k), r1_r.at[k, 0])
        push(half(t4 + 1, 0, k), half(t4 + 3, 0, k), r1_s.at[k, 2], r1_r.at[k, 2], r1m)
        got(blk(t4 + 2, k), r1_r.at[k, 1])
        push(half(t4 + 2, 1, k), half(t4 + 3, 1, k), r1_s.at[k, 3], r1_r.at[k, 3], r1p)

    def stage3(k):
        got(half(t4 + 3, 0, k), r1_r.at[k, 2])
        got(half(t4 + 3, 1, k), r1_r.at[k, 3])
        push(blk(t4, k, 4), blk(16 + t4, k, 4), r2_s.at[k, 1], r2_r.at[k, 1], r2p)
        push(blk(t4, k, 4), blk(8 + t4, k, 4), r2_s.at[k, 0], r2_r.at[k, 0], r2m)
        to_sibling(0, k)

    def stage4(k):
        got(blk(8 + t4, k, 4), r2_r.at[k, 0])
        push(blk(8 + t4, k, 2), blk(24 + t4, k, 2), r2_s.at[k, 2], r2_r.at[k, 2], r2m)
        got(blk(16 + t4, k, 4), r2_r.at[k, 1])
        push(blk(18 + t4, k, 2), blk(26 + t4, k, 2), r2_s.at[k, 3], r2_r.at[k, 3], r2p)
        to_sibling(1, k)
        to_sibling(2, k)

    def stage5(k):
        got(blk(24 + t4, k, 2), r2_r.at[k, 2])
        got(blk(26 + t4, k, 2), r2_r.at[k, 3])
        to_sibling(3, k)

    def select(k):
        for r2 in range(4):
            got(blk(r2 * 8 + u4, k, 4), sib_r.at[k, r2])
        start, size = PARTS[k]

        @pl.loop(0, size // 512)
        def _(n):
            off = pl.multiple_of(n * 512, 512)
            xsel[:, pl.ds(off, 512)] = jnp.dot(
                sel[...], pool[:, pl.ds(start + off, 512)], preferred_element_type=F32).astype(BF16)

    def multiply(k, lo, hi):
        start, size = PARTS[k]

        @pl.loop(lo // 256, hi // 256)
        def _(n):
            cols = pl.ds(pl.multiple_of(n * 256, 256), 256)
            out = lax.dot_general(xsel[:, 0:size], headv[cols, part(k)], (((1,), (1,)), ((), ())),
                                  preferred_element_type=F32)
            S[:, cols] = out if k == 0 else S[:, cols] + out

    def blocks(body):
        @pl.loop(0, rows_g // RB)
        def _(b):
            body(pl.multiple_of(b * RB, RB))

    def mine(gi, rows):
        return pl.ds(pl.multiple_of(gi * rows_g + rows, RB), RB)

    def cols_of(p):
        return slice(p * PIECE, (p + 1) * PIECE)

    def send_first(p):
        plus, minus = (0, 2) if p < 2 else (1, 0)

        def body(rows):
            r = pl.ds(rows, RB)
            for buf, scales, gi in ((SP, CP, plus), (SM, CM, minus)):
                coded, scale = quantize(S[mine(gi, rows), cols_of(p)])
                buf[r, cols_of(p)] = coded
                scales[p] += to_row(scale, 256, rows)

        blocks(body)
        push(SP.at[:, cols_of(p)], RM.at[:, cols_of(p)], rs_s.at[p, 0], rs_r.at[p, 0], zdev[1])
        push(SM.at[:, cols_of(p)], RP.at[:, cols_of(p)], rs_s.at[p, 1], rs_r.at[p, 1], zdev[3])
        push(CP.at[p], KM.at[p], rs_s.at[p, 2], rs_r.at[p, 2], zdev[1])
        push(CM.at[p], KP.at[p], rs_s.at[p, 3], rs_r.at[p, 3], zdev[3])

    def send_second(j):
        for p in (j, j + 2):
            got(RM.at[:, cols_of(p)], rs_r.at[p, 0])
            got(RP.at[:, cols_of(p)], rs_r.at[p, 1])
            got(KM.at[p], rs_r.at[p, 2])
            got(KP.at[p], rs_r.at[p, 3])

        def body(rows):
            r = pl.ds(rows, RB)
            for buf, scales, recv, rscale, gi, p in ((SP2, CP2, RM, KM, 1, j), (SM2, CM2, RP, KP, 2, j + 2)):
                old = widen(recv[r, cols_of(p)]) * to_col(rscale[p], RB, rows)
                coded, scale = quantize(S[mine(gi, rows), cols_of(p)] + old)
                buf[r, cols_of(j)] = coded
                scales[j] += to_row(scale, 256, rows)

        blocks(body)
        push(SP2.at[:, cols_of(j)], RM2.at[:, cols_of(j)], rt_s.at[j, 0], rt_r.at[j, 0], zdev[1])
        push(SM2.at[:, cols_of(j)], RP2.at[:, cols_of(j)], rt_s.at[j, 1], rt_r.at[j, 1], zdev[3])
        push(CP2.at[j], KM2.at[j], rt_s.at[j, 2], rt_r.at[j, 2], zdev[1])
        push(CM2.at[j], KP2.at[j], rt_s.at[j, 3], rt_r.at[j, 3], zdev[3])

    def finish(j):
        got(RM2.at[:, cols_of(j)], rt_r.at[j, 0])
        got(RP2.at[:, cols_of(j)], rt_r.at[j, 1])
        got(KM2.at[j], rt_r.at[j, 2])
        got(KP2.at[j], rt_r.at[j, 3])

        def body(rows):
            r = pl.ds(rows, RB)
            for p, near, nscale, far, fscale in ((j, RP, KP, RM2, KM2), (j + 2, RM, KM, RP2, KP2)):
                total = S[mine(3, rows), cols_of(p)]
                total += widen(near[r, cols_of(p)]) * to_col(nscale[p], RB, rows)
                total += widen(far[r, cols_of(j)]) * to_col(fscale[j], RB, rows)
                logits = total * row_scale[:, cols_of(p)]
                S[mine(3, rows), cols_of(p)] = logits
                top = jnp.max(logits, axis=1, keepdims=True)
                TA[0, p:p + 1, :] += to_row(top, 256, rows)
                TA[0, p + 4:p + 5, :] += to_row(jnp.sum(jnp.exp(logits - top), axis=1, keepdims=True), 256, rows)

        blocks(body)

    for i in range(n_parts + 2):
        if i < n_parts:
            stage1(i)
        if 0 <= i - 1 < n_parts:
            stage2(i - 1)
        if 0 <= i - 2:
            stage3(i - 2)
    stage4(0)
    stage4(1)
    for k in range(n_parts):
        stage5(k)
        select(k)
        if k + 2 < n_parts:
            stage4(k + 2)
        head_copies[k].wait()
        if k + 1 < n_parts:
            multiply(k, 0, voc)
    for p in (0, 2, 1, 3):
        multiply(n_parts - 1, p * PIECE, (p + 1) * PIECE)
        send_first(p)
    send_second(0)

    base = v * voc

    @pl.loop(0, rows_g // 32)
    def _(b):
        rows = pl.multiple_of(b * 32, 32)
        ids = [to_col(div[j:j + 1, :], 32, rows) - base for j in range(16)]
        for k in range(voc // 256):
            token = iota((32, 256), 1) + k * 256
            acc = jnp.zeros((32, 256), F32)
            for j in range(16):
                acc = acc - jnp.where(ids[j] == token, 0.5, 0.0)
            CN[pl.ds(rows, 32), k * 256:(k + 1) * 256] = acc

    send_second(1)

    for d in (1, 2, 3):
        got(st.at[(q + 4 - d) % 4], t_r.at[d - 1])
    replica, lane, depth, _ = row_info(order_of(q), live)
    slot_col = to_col(replica * slots + lane * 9 + depth, rows_g)
    score = jnp.zeros((rows_g, 1), F32)
    factor = jnp.zeros((rows_g, 1), F32)
    for r in range(4):
        hit = slot_col - r * slots == iota((rows_g, st.shape[2]), 1)
        score += jnp.sum(jnp.where(hit, st[r, 0:1, :], 0.0), axis=1, keepdims=True)
        factor += jnp.sum(jnp.where(hit, st[r, 1:2, :], 0.0), axis=1, keepdims=True)
    inverse = 1.0 / factor

    finish(0)
    finish(1)

    for i in range(1, 8):
        push(TA.at[0], TA.at[i], ta_s.at[i], ta_r.at[i], adev[i])

    def combine(tops, totals):
        top = functools.reduce(jnp.maximum, tops)
        return top, sum(total * jnp.exp(t - top) for t, total in zip(tops, totals))

    for i in range(1, 8):
        got(TA.at[i], ta_r.at[i])
    top, total = combine([TA[i, p:p + 1, :] for i in range(8) for p in range(4)],
                         [TA[i, p + 4:p + 5, :] for i in range(8) for p in range(4)])
    TB[0, 0:1, :] = top
    TB[0, 1:2, :] = total
    for i in range(1, 4):
        push(TB.at[0], TB.at[i], tb_s.at[i], tb_r.at[i], bdev[i])
    for i in range(1, 4):
        got(TB.at[i], tb_r.at[i])
    top, total = combine([TB[i, 0:1, :] for i in range(4)], [TB[i, 1:2, :] for i in range(4)])
    lse = to_col(top + jnp.log(total), rows_g)
    LS[q, 0:1, :] = to_row(lse, 256)
    for d in (1, 2, 3):
        push(LS.at[q], LS.at[q], ls_s.at[d - 1], ls_r.at[d - 1], zdev[d])
    shift = score - lse
    outs = []
    for p in range(voc // PIECE):
        CN[:, cols_of(p)] = (S[3 * rows_g:4 * rows_g, cols_of(p)] + CN[:, cols_of(p)] + shift) * inverse
        copy = pltpu.make_async_copy(CN.at[:, cols_of(p)], scored.at[:, cols_of(p)], out_sem.at[p])
        copy.start()
        outs.append(copy)

    for d in (1, 2, 3):
        got(LS.at[(q + 4 - d) % 4], ls_r.at[d - 1])
    acc = jnp.zeros((1, st.shape[2]), F32)
    for g in range(4):
        replica, lane, depth, _ = row_info(by_group[g], live)
        slot_col = to_col(replica * slots + lane * 9 + depth, rows_g)
        hit = slot_col - q * slots == iota((rows_g, st.shape[2]), 1)
        acc += jnp.sum(jnp.where(hit, to_col(LS[g, 0:1, :], rows_g), 0.0), axis=0, keepdims=True)
    slotn[...] = acc[:, 0:slots].reshape(slots)

    for copy in outs:
        copy.wait()
    for copy in sends:
        copy.wait_send()


def call(hidden, head, row_scale, live, order, blp, tlen, div):
    rows_g, voc, width, slots = div.shape[1], head.shape[0], head.shape[1], blp.shape[0]
    half_v = voc // 2
    n = len(PARTS)
    pieces = voc // PIECE
    dma = pltpu.SemaphoreType.DMA
    vmem = pl.BlockSpec(memory_space=pltpu.VMEM)
    anyspace = pl.BlockSpec(memory_space=pl.ANY)
    smem = pl.BlockSpec(memory_space=pltpu.SMEM)
    return pl.pallas_call(
        kernel,
        out_shape=(jax.ShapeDtypeStruct((rows_g, voc), F32), jax.ShapeDtypeStruct((slots,), F32)),
        in_specs=[anyspace, anyspace, vmem, smem, vmem, vmem, vmem, vmem],
        out_specs=(anyspace, vmem),
        scratch_shapes=[
            pltpu.VMEM((4, hidden.shape[0], width), BF16),
            pltpu.VMEM((32 * CAP, width), BF16),
            pltpu.VMEM((voc, width), BF16),
            pltpu.VMEM((4, 8, 384), F32),
            pltpu.VMEM((4 * rows_g, 32 * CAP), BF16),
            pltpu.VMEM((4 * rows_g, max(size for _, size in PARTS)), BF16),
            pltpu.VMEM((4 * rows_g, voc), F32),
            pltpu.VMEM((rows_g, voc), F32),
            *[pltpu.VMEM((rows_g, voc), I16)] * 4,
            *[pltpu.VMEM((rows_g, half_v), I16)] * 4,
            *[pltpu.VMEM((pieces, 1, 256), F32)] * 4,
            *[pltpu.VMEM((pieces // 2, 1, 256), F32)] * 4,
            pltpu.VMEM((8, 8, 256), F32),
            pltpu.VMEM((4, 8, 256), F32),
            pltpu.VMEM((4, 8, 256), F32),
            dma((n,)), dma((n,)), dma((pieces,)),
            dma((n, 3)), dma((n, 3)), dma((3,)), dma((3,)),
            dma((n, 4)), dma((n, 4)), dma((n, 4)), dma((n, 4)), dma((n, 4)), dma((n, 4)),
            dma((pieces, 4)), dma((pieces, 4)), dma((pieces // 2, 4)), dma((pieces // 2, 4)),
            dma((8,)), dma((8,)), dma((4,)), dma((4,)), dma((3,)), dma((3,)),
        ],
        compiler_params=pltpu.CompilerParams(
            collective_id=0, has_side_effects=True, vmem_limit_bytes=60 * 1024 * 1024),
    )(hidden, head, row_scale, live, order, blp, tlen, div)


def per_device(hidden, head, row_scale, live, order, beam_log_prob, token_length, div_ids):
    return call(hidden, head, row_scale[None, :], live, order, beam_log_prob, token_length, div_ids.T)


def solution(mesh):
    return jax.shard_map(
        per_device,
        mesh=mesh,
        in_specs=(
            P(("dp", "vocab"), None),
            P("vocab", "dp"),
            P("vocab"),
            P(),
            P(),
            P("dp"),
            P("dp"),
            P("dp", None),
        ),
        out_specs=(P("dp", "vocab"), P("dp")),
        check_vma=False,
    )
```

```python
import functools

import jax
import jax.numpy as jnp
from jax import lax
from jax.experimental import pallas as pl
from jax.experimental.pallas import tpu as pltpu
from jax.sharding import PartitionSpec as P

F32, BF16, I32, I16 = jnp.float32, jnp.bfloat16, jnp.int32, jnp.int16
MESH = pl.DeviceIdType.MESH

CAP = 32
RB = 96
PIECES = ((0, 256), (256, 256), (512, 512))


def iota(shape, axis):
    return lax.broadcasted_iota(I32, shape, axis)


def to_col(row, n, shift=0):
    width = row.shape[1]
    hit = iota((n, width), 0) + shift == iota((n, width), 1)
    return jnp.sum(jnp.where(hit, row, jnp.zeros_like(row)), axis=1, keepdims=True)


def to_row(col, width, shift=0):
    n = col.shape[0]
    hit = iota((n, width), 0) + shift == iota((n, width), 1)
    return jnp.sum(jnp.where(hit, col, jnp.zeros_like(col)), axis=0, keepdims=True)


def live_of_lane(count, lane):
    return (count - lane + 31) >> 5


def row_info(order, live):
    e0 = live[0]
    e1 = e0 + live[1]
    e2 = e1 + live[2]
    past = [(order >= e).astype(I32) for e in (e0, e1, e2)]
    replica = past[0] + past[1] + past[2]
    within = order - (past[0] * live[0] + past[1] * live[1] + past[2] * live[2])
    lane, depth = within & 31, within >> 5
    row = depth
    for i in range(3):
        row = row + past[i] * live_of_lane(live[i], lane)
    return replica, lane, depth, row


def place(lane, x, y):
    lx, ly, lc = lane >> 3, (lane >> 1) & 3, lane & 1
    dx, dy = (lx - x) & 3, (ly - y) & 3
    r1 = dx + lc * (dy - dx)
    r2 = dy + lc * (dx - dy)
    g1, g2 = r1 ^ (r1 >> 1), r2 ^ (r2 >> 1)
    near = (g2 == 1) | (g2 == 2)
    chunk = jnp.where(near, 1 + (g1 >> 1), g2)
    minor = jnp.where(near, (g2 - 1) * 2 + (g1 & 1), g1)
    return chunk * 8 + lc * 4 + minor


def quantize(val):
    top = jnp.maximum(jnp.max(jnp.abs(val), axis=1, keepdims=True), 1e-30)
    coded = jnp.round(val * (32767.0 / top)).astype(I32).astype(I16)
    return coded, top * (1.0 / 32767.0)


def widen(coded):
    return coded.astype(I32).astype(F32)


def kernel(hidden, head, row_scale, live, order, blp, tlen, div,
           scored, slotn,
           hrecv, pool, headv, st, sel, xsel, S, CN,
           SP, SM, RM, RP, SP2, SM2, RM2, RP2,
           CP, CM, KM, KP, CP2, CM2, KM2, KP2,
           TL, TA, TB, LS,
           head_sem, own_sem, out_sem, z_s, z_r, t_s, t_r,
           r1_s, r1_r, r2_s, r2_r, sib_s, sib_r,
           rs_s, rs_r, rt_s, rt_r, ta_s, ta_r, tb_s, tb_r, ls_s, ls_r):
    q = lax.axis_index("dp")
    v = lax.axis_index("vocab")
    x, y, c = v // 8, (v // 2) % 4, v % 2
    width = hidden.shape[1] // 4
    voc = head.shape[0]
    half_v = voc // 2
    rows_g = div.shape[1]
    slots = blp.shape[0]
    n_pieces = len(PIECES)

    def dev(zz, xx, yy, cc):
        return (zz % 4, (xx % 4) * 8 + (yy % 4) * 2 + (cc % 2))

    zdev = [dev(q + d, x, y, c) for d in range(4)]
    fan = [(dy, dc) for dy in range(4) for dc in range(2)]
    adev = [dev(q, x, y + dy, c + dc) for dy, dc in fan]
    bdev = [dev(q, x + d, y, c) for d in range(4)]
    sibling = adev[1]
    r1p = dev(q, x + (1 - c), y + c, c)
    r1m = dev(q, x + 3 * (1 - c), y + 3 * c, c)
    r1f = dev(q, x + 2 * (1 - c), y + 2 * c, c)
    r2p = dev(q, x + c, y + (1 - c), c)
    r2m = dev(q, x + 3 * c, y + 3 * (1 - c), c)
    sends = []

    def rc(src, dst, ss, rs, device):
        return pltpu.make_async_remote_copy(
            src_ref=src, dst_ref=dst, send_sem=ss, recv_sem=rs, device_id=device, device_id_type=MESH)

    def push(src, dst, ss, rs, device):
        copy = rc(src, dst, ss, rs, device)
        copy.start()
        sends.append(copy)

    def got(dst, rs):
        rc(dst, dst, t_s.at[0], rs, zdev[1]).wait_recv()

    barrier = pltpu.get_barrier_semaphore()
    peers = zdev[1:] + adev[1:] + bdev[1:]
    for device in peers:
        pl.semaphore_signal(barrier, inc=1, device_id=device, device_id_type=MESH)

    def quarter(group):
        return hidden.at[:, pl.ds(pl.multiple_of(group * width, 128), width)]

    own_copy = pltpu.make_async_copy(quarter(q), hrecv.at[q], own_sem)
    own_copy.start()
    head_copy = pltpu.make_async_copy(head, headv, head_sem)
    head_copy.start()
    st[q] = jnp.zeros(st.shape[1:], F32)
    st[q, 0:1, 0:slots] = blp[...].reshape(1, slots)
    lengths = tlen[...].reshape(1, slots).astype(F32)
    st[q, 1:2, 0:slots] = jnp.exp(0.8 * jnp.log((5.0 + lengths) / 6.0))
    for ref in (CP, CM, CP2, CM2):
        ref[...] = jnp.zeros(ref.shape, F32)
    TL[...] = jnp.zeros(TL.shape, F32)
    TA[0] = jnp.zeros(TA.shape[1:], F32)
    TB[0] = jnp.zeros(TB.shape[1:], F32)
    LS[q] = jnp.zeros(LS.shape[1:], F32)

    pl.semaphore_wait(barrier, len(peers))

    for d in (2, 1, 3):
        push(quarter((q + d) % 4), hrecv.at[q], z_s.at[d - 1], z_r.at[d - 1], zdev[d])
    for d in (1, 2, 3):
        push(st.at[q], st.at[q], t_s.at[d - 1], t_r.at[d - 1], zdev[d])

    numbers = order[...].reshape(1, 4 * rows_g)
    by_group = [numbers[:, g * rows_g:(g + 1) * rows_g] for g in range(4)]

    def order_of(group):
        return sum(jnp.where(group == g, by_group[g], 0) for g in range(4))

    for gi, group in enumerate(((q + 2) % 4, (q + 1) % 4, (q + 3) % 4, q)):
        _, lane, _, row = row_info(order_of(group), live)
        at = to_col(place(lane, x, y) * CAP + row, rows_g)
        for b in range(32 * CAP // 128):
            hit = at == iota((rows_g, 128), 1) + 128 * b
            sel[gi * rows_g:(gi + 1) * rows_g, b * 128:(b + 1) * 128] = jnp.where(hit, 1.0, 0.0).astype(BF16)

    counts = [live_of_lane(live[r], v) for r in range(4)]
    picks = []
    first = 0
    for r in range(4):
        i, j = iota((CAP, 9), 0), iota((CAP, 9), 1)
        picks.append(jnp.where((i == first + j) & (j < counts[r]), 1.0, 0.0).astype(BF16))
        first = first + counts[r]

    t4 = 4 * c
    u4 = 4 - t4

    def blk(idx):
        return pool.at[pl.ds(pl.multiple_of(idx * CAP, CAP), CAP), :]

    def half(idx, h):
        return pool.at[pl.ds(pl.multiple_of(idx * CAP + h * (CAP // 2), CAP // 2), CAP // 2), :]

    def to_sibling(ch, m):
        push(blk(ch * 8 + t4 + m), blk(ch * 8 + t4 + m), sib_s.at[ch * 4 + m], sib_r.at[ch * 4 + m], sibling)

    def from_sibling(ch):
        for m in range(4):
            got(blk(ch * 8 + u4 + m), sib_r.at[ch * 4 + m])

    def spread(m):
        ch, mm = 1 + (m >> 1), m & 1
        push(blk(t4 + m), blk(ch * 8 + t4 + 2 + mm), r2_s.at[2 * m + 1], r2_r.at[2 * m + 1], r2p)
        push(blk(t4 + m), blk(ch * 8 + t4 + mm), r2_s.at[2 * m], r2_r.at[2 * m], r2m)

    own_copy.wait()
    for d in (1, 3, 2):
        got(hrecv.at[(q + 4 - d) % 4], z_r.at[d - 1])
    for k in range(0, width, 1024):
        acc = jnp.zeros((CAP, 1024), F32)
        for r in range(4):
            acc += jnp.dot(picks[r], hrecv[r, :, k:k + 1024], preferred_element_type=F32)
        pool[pl.ds(pl.multiple_of(t4 * CAP, CAP), CAP), k:k + 1024] = acc.astype(BF16)

    push(blk(t4), blk(t4 + 3), r1_s.at[2], r1_r.at[2], r1f)
    push(blk(t4), blk(t4 + 2), r1_s.at[1], r1_r.at[1], r1p)
    push(blk(t4), blk(t4 + 1), r1_s.at[0], r1_r.at[0], r1m)
    to_sibling(0, 0)
    spread(0)
    for m in (1, 2, 3):
        got(blk(t4 + m), r1_r.at[m - 1])
        spread(m)
        to_sibling(0, m)

    def relay(ch):
        for mm in range(2):
            m = 2 * (ch - 1) + mm
            got(blk(ch * 8 + t4 + mm), r2_r.at[2 * m])
            push(half(ch * 8 + t4 + mm, 0), half(24 + t4 + m, 0), r2_s.at[8 + 2 * m], r2_r.at[8 + 2 * m], r2m)
            got(blk(ch * 8 + t4 + 2 + mm), r2_r.at[2 * m + 1])
            push(half(ch * 8 + t4 + 2 + mm, 1), half(24 + t4 + m, 1), r2_s.at[9 + 2 * m], r2_r.at[9 + 2 * m], r2p)
            to_sibling(ch, mm)
            to_sibling(ch, 2 + mm)

    def relay_far():
        for m in range(4):
            got(half(24 + t4 + m, 0), r2_r.at[8 + 2 * m])
            got(half(24 + t4 + m, 1), r2_r.at[9 + 2 * m])
            to_sibling(3, m)

    def select(lo, hi):
        @pl.loop(0, width // 512)
        def _(n):
            cols = pl.ds(pl.multiple_of(n * 512, 512), 512)
            got_rows = jnp.dot(sel[:, lo * 256:hi * 256], pool[lo * 256:hi * 256, cols], preferred_element_type=F32)
            xsel[:, cols] = (got_rows if lo == 0 else xsel[:, cols].astype(F32) + got_rows).astype(BF16)

    def multiply(p):
        start, size = piece(p)

        @pl.loop(start // 256, (start + size) // 256)
        def _(n):
            cols = pl.ds(pl.multiple_of(n * 256, 256), 256)
            S[:, cols] = lax.dot_general(xsel[...], headv[cols, :], (((1,), (1,)), ((), ())),
                                         preferred_element_type=F32)

    def blocks(body):
        @pl.loop(0, rows_g // RB)
        def _(b):
            body(pl.multiple_of(b * RB, RB))

    def mine(gi, rows):
        return pl.ds(pl.multiple_of(gi * rows_g + rows, 32), RB)

    def piece(p):
        start, size = PIECES[p % n_pieces]
        return start + (p // n_pieces) * half_v, size

    def cols_of(p):
        start, size = piece(p)
        return slice(start, start + size)

    def send_first(p):
        plus, minus = (0, 2) if p < n_pieces else (1, 0)

        def body(rows):
            r = pl.ds(rows, RB)
            for buf, scales, gi in ((SP, CP, plus), (SM, CM, minus)):
                coded, scale = quantize(S[mine(gi, rows), cols_of(p)])
                buf[r, cols_of(p)] = coded
                scales[p] += to_row(scale, 256, rows)

        blocks(body)
        push(SP.at[:, cols_of(p)], RM.at[:, cols_of(p)], rs_s.at[p, 0], rs_r.at[p, 0], zdev[1])
        push(SM.at[:, cols_of(p)], RP.at[:, cols_of(p)], rs_s.at[p, 1], rs_r.at[p, 1], zdev[3])
        push(CP.at[p], KM.at[p], rs_s.at[p, 2], rs_r.at[p, 2], zdev[1])
        push(CM.at[p], KP.at[p], rs_s.at[p, 3], rs_r.at[p, 3], zdev[3])

    def send_second(j):
        for p in (j, j + n_pieces):
            got(RM.at[:, cols_of(p)], rs_r.at[p, 0])
            got(RP.at[:, cols_of(p)], rs_r.at[p, 1])
            got(KM.at[p], rs_r.at[p, 2])
            got(KP.at[p], rs_r.at[p, 3])

        def body(rows):
            r = pl.ds(rows, RB)
            for buf, scales, recv, rscale, gi, p in ((SP2, CP2, RM, KM, 1, j), (SM2, CM2, RP, KP, 2, j + n_pieces)):
                old = widen(recv[r, cols_of(p)]) * to_col(rscale[p], RB, rows)
                coded, scale = quantize(S[mine(gi, rows), cols_of(p)] + old)
                buf[r, cols_of(j)] = coded
                scales[j] += to_row(scale, 256, rows)

        blocks(body)
        push(SP2.at[:, cols_of(j)], RM2.at[:, cols_of(j)], rt_s.at[j, 0], rt_r.at[j, 0], zdev[1])
        push(SM2.at[:, cols_of(j)], RP2.at[:, cols_of(j)], rt_s.at[j, 1], rt_r.at[j, 1], zdev[3])
        push(CP2.at[j], KM2.at[j], rt_s.at[j, 2], rt_r.at[j, 2], zdev[1])
        push(CM2.at[j], KP2.at[j], rt_s.at[j, 3], rt_r.at[j, 3], zdev[3])

    def finish(j):
        got(RM2.at[:, cols_of(j)], rt_r.at[j, 0])
        got(RP2.at[:, cols_of(j)], rt_r.at[j, 1])
        got(KM2.at[j], rt_r.at[j, 2])
        got(KP2.at[j], rt_r.at[j, 3])

        def body(rows):
            r = pl.ds(rows, RB)
            for p, near, nscale, far, fscale in ((j, RP, KP, RM2, KM2), (j + n_pieces, RM, KM, RP2, KP2)):
                total = S[mine(3, rows), cols_of(p)]
                total += widen(near[r, cols_of(p)]) * to_col(nscale[p], RB, rows)
                total += widen(far[r, cols_of(j)]) * to_col(fscale[j], RB, rows)
                logits = total * row_scale[:, cols_of(p)]
                S[mine(3, rows), cols_of(p)] = logits
                top = jnp.max(logits, axis=1, keepdims=True)
                TL[p:p + 1, :] += to_row(top, 256, rows)
                TL[p + 8:p + 9, :] += to_row(jnp.sum(jnp.exp(logits - top), axis=1, keepdims=True), 256, rows)

        blocks(body)

    base = v * voc

    @pl.loop(0, rows_g // 32)
    def _(b):
        rows = pl.multiple_of(b * 32, 32)
        ids = [to_col(div[j:j + 1, :], 32, rows) - base for j in range(16)]
        for k in range(voc // 256):
            token = iota((32, 256), 1) + k * 256
            acc = jnp.zeros((32, 256), F32)
            for j in range(16):
                acc = acc - jnp.where(ids[j] == token, 0.5, 0.0)
            CN[pl.ds(rows, 32), k * 256:(k + 1) * 256] = acc

    from_sibling(0)
    relay(1)
    from_sibling(1)
    select(0, 2)
    relay(2)
    from_sibling(2)
    select(2, 3)
    relay_far()
    from_sibling(3)
    select(3, 4)
    head_copy.wait()
    for j in range(n_pieces):
        for p in (j, j + n_pieces):
            multiply(p)
            send_first(p)
        if j >= 1:
            send_second(j - 1)
    send_second(n_pieces - 1)

    for d in (1, 2, 3):
        got(st.at[(q + 4 - d) % 4], t_r.at[d - 1])
    replica, lane, depth, _ = row_info(order_of(q), live)
    slot_col = to_col(replica * slots + lane * 9 + depth, rows_g)
    score = jnp.zeros((rows_g, 1), F32)
    factor = jnp.zeros((rows_g, 1), F32)
    for r in range(4):
        hit = slot_col - r * slots == iota((rows_g, st.shape[2]), 1)
        score += jnp.sum(jnp.where(hit, st[r, 0:1, :], 0.0), axis=1, keepdims=True)
        factor += jnp.sum(jnp.where(hit, st[r, 1:2, :], 0.0), axis=1, keepdims=True)
    inverse = 1.0 / factor

    for j in range(n_pieces):
        finish(j)

    def combine(tops, totals):
        top = functools.reduce(jnp.maximum, tops)
        return top, sum(total * jnp.exp(t - top) for t, total in zip(tops, totals))

    top, total = combine([TL[p:p + 1, :] for p in range(2 * n_pieces)], [TL[p + 8:p + 9, :] for p in range(2 * n_pieces)])
    TA[0, 0:1, :] = top
    TA[0, 1:2, :] = total
    for i in range(1, 8):
        push(TA.at[0], TA.at[i], ta_s.at[i], ta_r.at[i], adev[i])
    for i in range(1, 8):
        got(TA.at[i], ta_r.at[i])
    top, total = combine([TA[i, 0:1, :] for i in range(8)], [TA[i, 1:2, :] for i in range(8)])
    TB[0, 0:1, :] = top
    TB[0, 1:2, :] = total
    for i in range(1, 4):
        push(TB.at[0], TB.at[i], tb_s.at[i], tb_r.at[i], bdev[i])
    for i in range(1, 4):
        got(TB.at[i], tb_r.at[i])
    top, total = combine([TB[i, 0:1, :] for i in range(4)], [TB[i, 1:2, :] for i in range(4)])
    lse = to_col(top + jnp.log(total), rows_g)
    LS[q, 0:1, :] = to_row(lse, 256)
    for d in (1, 2, 3):
        push(LS.at[q], LS.at[q], ls_s.at[d - 1], ls_r.at[d - 1], zdev[d])
    shift = score - lse
    outs = []
    for p in range(2 * n_pieces):
        CN[:, cols_of(p)] = (S[3 * rows_g:4 * rows_g, cols_of(p)] + CN[:, cols_of(p)] + shift) * inverse
        copy = pltpu.make_async_copy(CN.at[:, cols_of(p)], scored.at[:, cols_of(p)], out_sem.at[p])
        copy.start()
        outs.append(copy)

    for d in (1, 2, 3):
        got(LS.at[(q + 4 - d) % 4], ls_r.at[d - 1])
    acc = jnp.zeros((1, st.shape[2]), F32)
    for g in range(4):
        replica, lane, depth, _ = row_info(by_group[g], live)
        slot_col = to_col(replica * slots + lane * 9 + depth, rows_g)
        hit = slot_col - q * slots == iota((rows_g, st.shape[2]), 1)
        acc += jnp.sum(jnp.where(hit, to_col(LS[g, 0:1, :], rows_g), 0.0), axis=0, keepdims=True)
    slotn[...] = acc[:, 0:slots].reshape(slots)

    for copy in outs:
        copy.wait()
    for copy in sends:
        copy.wait_send()


def call(hidden, head, row_scale, live, order, blp, tlen, div):
    rows_g, voc, width, slots = div.shape[1], head.shape[0], head.shape[1], blp.shape[0]
    half_v = voc // 2
    n = 2 * len(PIECES)
    dma = pltpu.SemaphoreType.DMA
    vmem = pl.BlockSpec(memory_space=pltpu.VMEM)
    anyspace = pl.BlockSpec(memory_space=pl.ANY)
    smem = pl.BlockSpec(memory_space=pltpu.SMEM)
    return pl.pallas_call(
        kernel,
        out_shape=(jax.ShapeDtypeStruct((rows_g, voc), F32), jax.ShapeDtypeStruct((slots,), F32)),
        in_specs=[anyspace, anyspace, vmem, smem, vmem, vmem, vmem, vmem],
        out_specs=(anyspace, vmem),
        scratch_shapes=[
            pltpu.VMEM((4, hidden.shape[0], width), BF16),
            pltpu.VMEM((32 * CAP, width), BF16),
            pltpu.VMEM((voc, width), BF16),
            pltpu.VMEM((4, 8, 384), F32),
            pltpu.VMEM((4 * rows_g, 32 * CAP), BF16),
            pltpu.VMEM((4 * rows_g, width), BF16),
            pltpu.VMEM((4 * rows_g, voc), F32),
            pltpu.VMEM((rows_g, voc), F32),
            *[pltpu.VMEM((rows_g, voc), I16)] * 4,
            *[pltpu.VMEM((rows_g, half_v), I16)] * 4,
            *[pltpu.VMEM((n, 1, 256), F32)] * 4,
            *[pltpu.VMEM((n // 2, 1, 256), F32)] * 4,
            pltpu.VMEM((16, 256), F32),
            pltpu.VMEM((8, 8, 256), F32),
            pltpu.VMEM((4, 8, 256), F32),
            pltpu.VMEM((4, 8, 256), F32),
            dma, dma, dma((n,)),
            dma((3,)), dma((3,)), dma((3,)), dma((3,)),
            dma((3,)), dma((3,)), dma((16,)), dma((16,)), dma((16,)), dma((16,)),
            dma((n, 4)), dma((n, 4)), dma((n // 2, 4)), dma((n // 2, 4)),
            dma((8,)), dma((8,)), dma((4,)), dma((4,)), dma((3,)), dma((3,)),
        ],
        compiler_params=pltpu.CompilerParams(
            collective_id=0, has_side_effects=True, vmem_limit_bytes=60 * 1024 * 1024),
    )(hidden, head, row_scale, live, order, blp, tlen, div)


def per_device(hidden, head, row_scale, live, order, beam_log_prob, token_length, div_ids):
    return call(hidden, head, row_scale[None, :], live, order, beam_log_prob, token_length, div_ids.T)


def solution(mesh):
    return jax.shard_map(
        per_device,
        mesh=mesh,
        in_specs=(
            P(("dp", "vocab"), None),
            P("vocab", "dp"),
            P("vocab"),
            P(),
            P(),
            P("dp"),
            P("dp"),
            P("dp", None),
        ),
        out_specs=(P("dp", "vocab"), P("dp")),
        check_vma=False,
    )
```

```python
import functools

import jax
import jax.numpy as jnp
from jax import lax
from jax.experimental import pallas as pl
from jax.experimental.pallas import tpu as pltpu
from jax.sharding import PartitionSpec as P

F32, BF16, I32, I16 = jnp.float32, jnp.bfloat16, jnp.int32, jnp.int16
MESH = pl.DeviceIdType.MESH

CAP = 32
RB = 96
PIECES = ((0, 256), (256, 512), (768, 256))


def iota(shape, axis):
    return lax.broadcasted_iota(I32, shape, axis)


def to_col(row, n, shift=0):
    width = row.shape[1]
    hit = iota((n, width), 0) + shift == iota((n, width), 1)
    return jnp.sum(jnp.where(hit, row, jnp.zeros_like(row)), axis=1, keepdims=True)


def to_row(col, width, shift=0):
    n = col.shape[0]
    hit = iota((n, width), 0) + shift == iota((n, width), 1)
    return jnp.sum(jnp.where(hit, col, jnp.zeros_like(col)), axis=0, keepdims=True)


def live_of_lane(count, lane):
    return (count - lane + 31) >> 5


def row_info(order, live):
    e0 = live[0]
    e1 = e0 + live[1]
    e2 = e1 + live[2]
    past = [(order >= e).astype(I32) for e in (e0, e1, e2)]
    replica = past[0] + past[1] + past[2]
    within = order - (past[0] * live[0] + past[1] * live[1] + past[2] * live[2])
    lane, depth = within & 31, within >> 5
    row = depth
    for i in range(3):
        row = row + past[i] * live_of_lane(live[i], lane)
    return replica, lane, depth, row


def place(lane, x, y):
    lx, ly, lc = lane >> 3, (lane >> 1) & 3, lane & 1
    dx, dy = (lx - x) & 3, (ly - y) & 3
    r1 = dx + lc * (dy - dx)
    r2 = dy + lc * (dx - dy)
    g1, g2 = r1 ^ (r1 >> 1), r2 ^ (r2 >> 1)
    near = (g2 == 1) | (g2 == 2)
    chunk = jnp.where(near, 1 + (g1 >> 1), g2)
    minor = jnp.where(near, (g2 - 1) * 2 + (g1 & 1), g1)
    return chunk * 8 + lc * 4 + minor


def quantize(val):
    top = jnp.maximum(jnp.max(jnp.abs(val), axis=1, keepdims=True), 1e-30)
    coded = jnp.round(val * (32767.0 / top)).astype(I32).astype(I16)
    return coded, top * (1.0 / 32767.0)


def widen(coded):
    return coded.astype(I32).astype(F32)


def kernel(hidden, head, row_scale, live, order, blp, tlen, div,
           scored, slotn,
           slotv, row8, fold, folded, pool, headv, st, sel, xsel, S, CN,
           SP, SM, RM, RP, SP2, SM2, RM2, RP2,
           CP, CM, KM, KP, CP2, CM2, KM2, KP2,
           TL, TA, TB, LS,
           head_sem, own_sem, out_sem, z_s, z_r, t_s, t_r,
           r1_s, r1_r, r2_s, r2_r, sib_s, sib_r,
           rs_s, rs_r, rt_s, rt_r, ta_s, ta_r, tb_s, tb_r, ls_s, ls_r):
    q = lax.axis_index("dp")
    v = lax.axis_index("vocab")
    x, y, c = v // 8, (v // 2) % 4, v % 2
    width = hidden.shape[1] // 4
    voc = head.shape[0]
    half_v = voc // 2
    rows_g = div.shape[1]
    slots = blp.shape[0]
    n_pieces = len(PIECES)

    def dev(zz, xx, yy, cc):
        return (zz % 4, (xx % 4) * 8 + (yy % 4) * 2 + (cc % 2))

    zdev = [dev(q + d, x, y, c) for d in range(4)]
    fan = [(dy, dc) for dy in range(4) for dc in range(2)]
    adev = [dev(q, x, y + dy, c + dc) for dy, dc in fan]
    bdev = [dev(q, x + d, y, c) for d in range(4)]
    sibling = adev[1]
    r1p = dev(q, x + (1 - c), y + c, c)
    r1m = dev(q, x + 3 * (1 - c), y + 3 * c, c)
    r2p = dev(q, x + c, y + (1 - c), c)
    r2m = dev(q, x + 3 * c, y + 3 * (1 - c), c)
    sends = []

    def rc(src, dst, ss, rs, device):
        return pltpu.make_async_remote_copy(
            src_ref=src, dst_ref=dst, send_sem=ss, recv_sem=rs, device_id=device, device_id_type=MESH)

    def push(src, dst, ss, rs, device):
        copy = rc(src, dst, ss, rs, device)
        copy.start()
        sends.append(copy)

    def got(dst, rs):
        rc(dst, dst, t_s.at[0], rs, zdev[1]).wait_recv()

    barrier = pltpu.get_barrier_semaphore()
    peers = zdev[1:] + adev[1:] + bdev[1:]
    for device in peers:
        pl.semaphore_signal(barrier, inc=1, device_id=device, device_id_type=MESH)

    own_copy = pltpu.make_async_copy(hidden, slotv, own_sem)
    own_copy.start()
    head_copy = pltpu.make_async_copy(head, headv, head_sem)
    head_copy.start()
    st[q] = jnp.zeros(st.shape[1:], F32)
    st[q, 0:1, 0:slots] = blp[...].reshape(1, slots)
    lengths = tlen[...].reshape(1, slots).astype(F32)
    st[q, 1:2, 0:slots] = jnp.exp(0.8 * jnp.log((5.0 + lengths) / 6.0))
    for ref in (CP, CM, CP2, CM2):
        ref[...] = jnp.zeros(ref.shape, F32)
    TL[...] = jnp.zeros(TL.shape, F32)
    TA[0] = jnp.zeros(TA.shape[1:], F32)
    TB[0] = jnp.zeros(TB.shape[1:], F32)
    LS[q] = jnp.zeros(LS.shape[1:], F32)

    own_copy.wait()
    run, hw = width // 16, width // 2
    for g in range(4):
        nine = slotv[:, g * width:(g + 1) * width].astype(F32)
        fold[g * 16:(g + 1) * 16, 0:hw] = jnp.concatenate([nine[0:8, 0:hw], nine[0:8, hw:width]], axis=0).astype(BF16)
        for i in range(16):
            row8[i:i + 1, :] = nine[8:9, i * run:(i + 1) * run]
        fold[g * 16:(g + 1) * 16, hw:hw + run] = row8[...].astype(BF16)

    def rows16(ref, group):
        return ref.at[pl.ds(pl.multiple_of(group * 16, 16), 16), :]

    keep = pltpu.make_async_copy(rows16(fold, q), rows16(folded, q), own_sem)
    keep.start()

    pl.semaphore_wait(barrier, len(peers))

    for d in (2, 1, 3):
        push(rows16(fold, (q + d) % 4), rows16(folded, q), z_s.at[d - 1], z_r.at[d - 1], zdev[d])
    for d in (1, 2, 3):
        push(st.at[q], st.at[q], t_s.at[d - 1], t_r.at[d - 1], zdev[d])

    numbers = order[...].reshape(1, 4 * rows_g)
    by_group = [numbers[:, g * rows_g:(g + 1) * rows_g] for g in range(4)]

    def order_of(group):
        return sum(jnp.where(group == g, by_group[g], 0) for g in range(4))

    for gi, group in enumerate(((q + 2) % 4, (q + 1) % 4, (q + 3) % 4, q)):
        _, lane, _, row = row_info(order_of(group), live)
        at = to_col(place(lane, x, y) * CAP + row, rows_g)
        for b in range(32 * CAP // 128):
            hit = at == iota((rows_g, 128), 1) + 128 * b
            sel[gi * rows_g:(gi + 1) * rows_g, b * 128:(b + 1) * 128] = jnp.where(hit, 1.0, 0.0).astype(BF16)

    base = v * voc

    @pl.loop(0, rows_g // 32)
    def _(b):
        rows = pl.multiple_of(b * 32, 32)
        ids = [to_col(div[j:j + 1, :], 32, rows) - base for j in range(16)]
        for k in range(voc // 256):
            token = iota((32, 256), 1) + k * 256
            acc = jnp.zeros((32, 256), F32)
            for j in range(16):
                acc = acc - jnp.where(ids[j] == token, 0.5, 0.0)
            CN[pl.ds(rows, 32), k * 256:(k + 1) * 256] = acc

    counts = [live_of_lane(live[r], v) for r in range(4)]
    firsts = [0]
    for r in range(3):
        firsts.append(firsts[-1] + counts[r])

    def by_replica(values, r):
        return sum(jnp.where(r == i, values[i], 0) for i in range(4))

    i, j = iota((2 * CAP, 64), 0), iota((2 * CAP, 64), 1)
    replica, depth = j >> 4, j & 7
    hit = ((i >> 5) == ((j >> 3) & 1)) & ((i & 31) == by_replica(firsts, replica) + depth)
    pick = jnp.where(hit & (depth < by_replica(counts, replica)), 1.0, 0.0).astype(BF16)
    i, j = iota((16 * CAP, 64), 0), iota((16 * CAP, 64), 1)
    replica = j >> 4
    hit = ((i >> 5) == (j & 15)) & ((i & 31) == by_replica(firsts, replica) + 8)
    pick8 = jnp.where(hit & (by_replica(counts, replica) > 8), 1.0, 0.0).astype(BF16)

    t4 = 4 * c
    u4 = 4 - t4

    def blk(idx):
        return pool.at[pl.ds(pl.multiple_of(idx * CAP, CAP), CAP), :]

    def half(idx, h):
        return pool.at[pl.ds(pl.multiple_of(idx * CAP + h * (CAP // 2), CAP // 2), CAP // 2), :]

    def to_sibling(ch, m):
        push(blk(ch * 8 + t4 + m), blk(ch * 8 + t4 + m), sib_s.at[ch * 4 + m], sib_r.at[ch * 4 + m], sibling)

    def from_sibling(ch):
        for m in range(4):
            got(blk(ch * 8 + u4 + m), sib_r.at[ch * 4 + m])

    def spread(m):
        ch, mm = 1 + (m >> 1), m & 1
        push(blk(t4 + m), blk(ch * 8 + t4 + 2 + mm), r2_s.at[2 * m + 1], r2_r.at[2 * m + 1], r2p)
        push(blk(t4 + m), blk(ch * 8 + t4 + mm), r2_s.at[2 * m], r2_r.at[2 * m], r2m)

    keep.wait()
    for d in (1, 3, 2):
        got(rows16(folded, (q + 4 - d) % 4), z_r.at[d - 1])
    ninth = jnp.dot(pick8, folded[:, hw:hw + run], preferred_element_type=F32)
    for k in range(0, hw, 1024):
        both = jnp.dot(pick, folded[:, k:k + 1024], preferred_element_type=F32)
        for h in range(2):
            for n in range(0, 1024, run):
                at = h * hw + k + n
                b = at // run
                block = both[h * CAP:(h + 1) * CAP, n:n + run] + ninth[b * CAP:(b + 1) * CAP, :]
                pool[pl.ds(pl.multiple_of(t4 * CAP, CAP), CAP), at:at + run] = block.astype(BF16)

    push(blk(t4), blk(t4 + 2), r1_s.at[1], r1_r.at[1], r1p)
    push(blk(t4), blk(t4 + 1), r1_s.at[0], r1_r.at[0], r1m)
    to_sibling(0, 0)
    spread(0)
    got(blk(t4 + 1), r1_r.at[0])
    push(half(t4 + 1, 0), half(t4 + 3, 0), r1_s.at[2], r1_r.at[2], r1m)
    got(blk(t4 + 2), r1_r.at[1])
    push(half(t4 + 2, 1), half(t4 + 3, 1), r1_s.at[3], r1_r.at[3], r1p)
    spread(1)
    spread(2)
    to_sibling(0, 1)
    to_sibling(0, 2)
    got(half(t4 + 3, 0), r1_r.at[2])
    got(half(t4 + 3, 1), r1_r.at[3])
    spread(3)
    to_sibling(0, 3)

    def relay(m):
        ch, mm = 1 + (m >> 1), m & 1
        got(blk(ch * 8 + t4 + mm), r2_r.at[2 * m])
        push(half(ch * 8 + t4 + mm, 0), half(24 + t4 + m, 0), r2_s.at[8 + 2 * m], r2_r.at[8 + 2 * m], r2m)
        got(blk(ch * 8 + t4 + 2 + mm), r2_r.at[2 * m + 1])
        push(half(ch * 8 + t4 + 2 + mm, 1), half(24 + t4 + m, 1), r2_s.at[9 + 2 * m], r2_r.at[9 + 2 * m], r2p)
        to_sibling(ch, mm)
        to_sibling(ch, 2 + mm)

    def relay_far(first):
        for m in (first, first + 1):
            got(half(24 + t4 + m, 0), r2_r.at[8 + 2 * m])
            got(half(24 + t4 + m, 1), r2_r.at[9 + 2 * m])
            to_sibling(3, m)

    def select(lo, hi):
        @pl.loop(0, width // 512)
        def _(n):
            cols = pl.ds(pl.multiple_of(n * 512, 512), 512)
            got_rows = jnp.dot(sel[:, lo * 256:hi * 256], pool[lo * 256:hi * 256, cols], preferred_element_type=F32)
            xsel[:, cols] = (got_rows if lo == 0 else xsel[:, cols].astype(F32) + got_rows).astype(BF16)

    def multiply(start, size, lo, hi):
        @pl.loop(start // 256, (start + size) // 256)
        def _(n):
            cols = pl.ds(pl.multiple_of(n * 256, 256), 256)
            S[lo:hi, cols] = lax.dot_general(xsel[lo:hi, :], headv[cols, :], (((1,), (1,)), ((), ())),
                                             preferred_element_type=F32)

    def blocks(body):
        @pl.loop(0, rows_g // RB)
        def _(b):
            body(pl.multiple_of(b * RB, RB))

    def mine(gi, rows):
        return pl.ds(pl.multiple_of(gi * rows_g + rows, 32), RB)

    def piece(p):
        start, size = PIECES[p % n_pieces]
        return start + (p // n_pieces) * half_v, size

    def cols_of(p):
        start, size = piece(p)
        return slice(start, start + size)

    def send_first(p):
        plus, minus = (0, 2) if p < n_pieces else (1, 0)

        def body(rows):
            r = pl.ds(rows, RB)
            for buf, scales, gi in ((SP, CP, plus), (SM, CM, minus)):
                coded, scale = quantize(S[mine(gi, rows), cols_of(p)])
                buf[r, cols_of(p)] = coded
                scales[p] += to_row(scale, 256, rows)

        blocks(body)
        push(SP.at[:, cols_of(p)], RM.at[:, cols_of(p)], rs_s.at[p, 0], rs_r.at[p, 0], zdev[1])
        push(SM.at[:, cols_of(p)], RP.at[:, cols_of(p)], rs_s.at[p, 1], rs_r.at[p, 1], zdev[3])
        push(CP.at[p], KM.at[p], rs_s.at[p, 2], rs_r.at[p, 2], zdev[1])
        push(CM.at[p], KP.at[p], rs_s.at[p, 3], rs_r.at[p, 3], zdev[3])

    def send_second(j):
        for p in (j, j + n_pieces):
            got(RM.at[:, cols_of(p)], rs_r.at[p, 0])
            got(RP.at[:, cols_of(p)], rs_r.at[p, 1])
            got(KM.at[p], rs_r.at[p, 2])
            got(KP.at[p], rs_r.at[p, 3])

        def body(rows):
            r = pl.ds(rows, RB)
            for buf, scales, recv, rscale, gi, p in ((SP2, CP2, RM, KM, 1, j), (SM2, CM2, RP, KP, 2, j + n_pieces)):
                old = widen(recv[r, cols_of(p)]) * to_col(rscale[p], RB, rows)
                coded, scale = quantize(S[mine(gi, rows), cols_of(p)] + old)
                buf[r, cols_of(j)] = coded
                scales[j] += to_row(scale, 256, rows)

        blocks(body)
        push(SP2.at[:, cols_of(j)], RM2.at[:, cols_of(j)], rt_s.at[j, 0], rt_r.at[j, 0], zdev[1])
        push(SM2.at[:, cols_of(j)], RP2.at[:, cols_of(j)], rt_s.at[j, 1], rt_r.at[j, 1], zdev[3])
        push(CP2.at[j], KM2.at[j], rt_s.at[j, 2], rt_r.at[j, 2], zdev[1])
        push(CM2.at[j], KP2.at[j], rt_s.at[j, 3], rt_r.at[j, 3], zdev[3])

    def finish(j):
        got(RM2.at[:, cols_of(j)], rt_r.at[j, 0])
        got(RP2.at[:, cols_of(j)], rt_r.at[j, 1])
        got(KM2.at[j], rt_r.at[j, 2])
        got(KP2.at[j], rt_r.at[j, 3])

        def body(rows):
            r = pl.ds(rows, RB)
            for p, near, nscale, far, fscale in ((j, RP, KP, RM2, KM2), (j + n_pieces, RM, KM, RP2, KP2)):
                total = S[mine(3, rows), cols_of(p)]
                total += widen(near[r, cols_of(p)]) * to_col(nscale[p], RB, rows)
                total += widen(far[r, cols_of(j)]) * to_col(fscale[j], RB, rows)
                logits = total * row_scale[:, cols_of(p)]
                S[mine(3, rows), cols_of(p)] = logits
                top = jnp.max(logits, axis=1, keepdims=True)
                TL[p:p + 1, :] += to_row(top, 256, rows)
                TL[p + 8:p + 9, :] += to_row(jnp.sum(jnp.exp(logits - top), axis=1, keepdims=True), 256, rows)

        blocks(body)

    relay(0)
    from_sibling(0)
    select(0, 1)
    relay(1)
    relay(2)
    from_sibling(1)
    relay(3)
    from_sibling(2)
    relay_far(0)
    select(1, 3)
    relay_far(2)
    from_sibling(3)
    select(3, 4)
    head_copy.wait()

    others = 3 * rows_g
    for j in range(n_pieces):
        for p in (j, j + n_pieces):
            multiply(*piece(p), 0, others)
            send_first(p)
        if j >= 1:
            send_second(j - 1)
    multiply(0, half_v, others, 4 * rows_g)
    send_second(n_pieces - 1)
    multiply(half_v, half_v, others, 4 * rows_g)

    for d in (1, 2, 3):
        got(st.at[(q + 4 - d) % 4], t_r.at[d - 1])
    replica, lane, depth, _ = row_info(order_of(q), live)
    slot_col = to_col(replica * slots + lane * 9 + depth, rows_g)
    score = jnp.zeros((rows_g, 1), F32)
    factor = jnp.zeros((rows_g, 1), F32)
    for r in range(4):
        hit = slot_col - r * slots == iota((rows_g, st.shape[2]), 1)
        score += jnp.sum(jnp.where(hit, st[r, 0:1, :], 0.0), axis=1, keepdims=True)
        factor += jnp.sum(jnp.where(hit, st[r, 1:2, :], 0.0), axis=1, keepdims=True)
    inverse = 1.0 / factor

    for j in range(n_pieces):
        finish(j)

    def combine(tops, totals):
        top = functools.reduce(jnp.maximum, tops)
        return top, sum(total * jnp.exp(t - top) for t, total in zip(tops, totals))

    top, total = combine([TL[p:p + 1, :] for p in range(2 * n_pieces)], [TL[p + 8:p + 9, :] for p in range(2 * n_pieces)])
    TA[0, 0:1, :] = top
    TA[0, 1:2, :] = total
    for i in range(1, 8):
        push(TA.at[0], TA.at[i], ta_s.at[i], ta_r.at[i], adev[i])
    for i in range(1, 8):
        got(TA.at[i], ta_r.at[i])
    top, total = combine([TA[i, 0:1, :] for i in range(8)], [TA[i, 1:2, :] for i in range(8)])
    TB[0, 0:1, :] = top
    TB[0, 1:2, :] = total
    for i in range(1, 4):
        push(TB.at[0], TB.at[i], tb_s.at[i], tb_r.at[i], bdev[i])
    for i in range(1, 4):
        got(TB.at[i], tb_r.at[i])
    top, total = combine([TB[i, 0:1, :] for i in range(4)], [TB[i, 1:2, :] for i in range(4)])
    lse = to_col(top + jnp.log(total), rows_g)
    LS[q, 0:1, :] = to_row(lse, 256)
    for d in (1, 2, 3):
        push(LS.at[q], LS.at[q], ls_s.at[d - 1], ls_r.at[d - 1], zdev[d])
    shift = score - lse
    outs = []
    for p in range(2 * n_pieces):
        CN[:, cols_of(p)] = (S[3 * rows_g:4 * rows_g, cols_of(p)] + CN[:, cols_of(p)] + shift) * inverse
        copy = pltpu.make_async_copy(CN.at[:, cols_of(p)], scored.at[:, cols_of(p)], out_sem.at[p])
        copy.start()
        outs.append(copy)

    for d in (1, 2, 3):
        got(LS.at[(q + 4 - d) % 4], ls_r.at[d - 1])
    acc = jnp.zeros((1, st.shape[2]), F32)
    for g in range(4):
        replica, lane, depth, _ = row_info(by_group[g], live)
        slot_col = to_col(replica * slots + lane * 9 + depth, rows_g)
        hit = slot_col - q * slots == iota((rows_g, st.shape[2]), 1)
        acc += jnp.sum(jnp.where(hit, to_col(LS[g, 0:1, :], rows_g), 0.0), axis=0, keepdims=True)
    slotn[...] = acc[:, 0:slots].reshape(slots)

    for copy in outs:
        copy.wait()
    for copy in sends:
        copy.wait_send()


def call(hidden, head, row_scale, live, order, blp, tlen, div):
    rows_g, voc, width, slots = div.shape[1], head.shape[0], head.shape[1], blp.shape[0]
    half_v = voc // 2
    n = 2 * len(PIECES)
    dma = pltpu.SemaphoreType.DMA
    vmem = pl.BlockSpec(memory_space=pltpu.VMEM)
    anyspace = pl.BlockSpec(memory_space=pl.ANY)
    smem = pl.BlockSpec(memory_space=pltpu.SMEM)
    return pl.pallas_call(
        kernel,
        out_shape=(jax.ShapeDtypeStruct((rows_g, voc), F32), jax.ShapeDtypeStruct((slots,), F32)),
        in_specs=[anyspace, anyspace, vmem, smem, vmem, vmem, vmem, vmem],
        out_specs=(anyspace, vmem),
        scratch_shapes=[
            pltpu.VMEM(hidden.shape, BF16),
            pltpu.VMEM((16, width // 16), F32),
            pltpu.VMEM((64, width // 2 + width // 16), BF16),
            pltpu.VMEM((64, width // 2 + width // 16), BF16),
            pltpu.VMEM((32 * CAP, width), BF16),
            pltpu.VMEM((voc, width), BF16),
            pltpu.VMEM((4, 8, 384), F32),
            pltpu.VMEM((4 * rows_g, 32 * CAP), BF16),
            pltpu.VMEM((4 * rows_g, width), BF16),
            pltpu.VMEM((4 * rows_g, voc), F32),
            pltpu.VMEM((rows_g, voc), F32),
            *[pltpu.VMEM((rows_g, voc), I16)] * 4,
            *[pltpu.VMEM((rows_g, half_v), I16)] * 4,
            *[pltpu.VMEM((n, 1, 256), F32)] * 4,
            *[pltpu.VMEM((n // 2, 1, 256), F32)] * 4,
            pltpu.VMEM((16, 256), F32),
            pltpu.VMEM((8, 8, 256), F32),
            pltpu.VMEM((4, 8, 256), F32),
            pltpu.VMEM((4, 8, 256), F32),
            dma, dma, dma((n,)),
            dma((3,)), dma((3,)), dma((3,)), dma((3,)),
            dma((4,)), dma((4,)), dma((16,)), dma((16,)), dma((16,)), dma((16,)),
            dma((n, 4)), dma((n, 4)), dma((n // 2, 4)), dma((n // 2, 4)),
            dma((8,)), dma((8,)), dma((4,)), dma((4,)), dma((3,)), dma((3,)),
        ],
        compiler_params=pltpu.CompilerParams(
            collective_id=0, has_side_effects=True, vmem_limit_bytes=60 * 1024 * 1024),
    )(hidden, head, row_scale, live, order, blp, tlen, div)


def per_device(hidden, head, row_scale, live, order, beam_log_prob, token_length, div_ids):
    return call(hidden, head, row_scale[None, :], live, order, beam_log_prob, token_length, div_ids.T)


def solution(mesh):
    return jax.shard_map(
        per_device,
        mesh=mesh,
        in_specs=(
            P(("dp", "vocab"), None),
            P("vocab", "dp"),
            P("vocab"),
            P(),
            P(),
            P("dp"),
            P("dp"),
            P("dp", None),
        ),
        out_specs=(P("dp", "vocab"), P("dp")),
        check_vma=False,
    )
```

```python
import functools

import jax
import jax.numpy as jnp
from jax import lax
from jax.experimental import pallas as pl
from jax.experimental.pallas import tpu as pltpu
from jax.sharding import PartitionSpec as P

F32, BF16, I32, I16 = jnp.float32, jnp.bfloat16, jnp.int32, jnp.int16
MESH = pl.DeviceIdType.MESH

CAP = 32
RB = 192
PIECES = ((0, 256), (256, 512), (768, 256))


def iota(shape, axis):
    return lax.broadcasted_iota(I32, shape, axis)


def to_col(row, n, shift=0):
    width = row.shape[1]
    hit = iota((n, width), 0) + shift == iota((n, width), 1)
    return jnp.sum(jnp.where(hit, row, jnp.zeros_like(row)), axis=1, keepdims=True)


def to_row(col, width, shift=0):
    n = col.shape[0]
    hit = iota((n, width), 0) + shift == iota((n, width), 1)
    return jnp.sum(jnp.where(hit, col, jnp.zeros_like(col)), axis=0, keepdims=True)


def live_of_lane(count, lane):
    return (count - lane + 31) >> 5


def row_info(order, live):
    e0 = live[0]
    e1 = e0 + live[1]
    e2 = e1 + live[2]
    past = [(order >= e).astype(I32) for e in (e0, e1, e2)]
    replica = past[0] + past[1] + past[2]
    within = order - (past[0] * live[0] + past[1] * live[1] + past[2] * live[2])
    lane, depth = within & 31, within >> 5
    row = depth
    for i in range(3):
        row = row + past[i] * live_of_lane(live[i], lane)
    return replica, lane, depth, row


def place(lane, x, y):
    lx, ly, lc = lane >> 3, (lane >> 1) & 3, lane & 1
    dx, dy = (lx - x) & 3, (ly - y) & 3
    r1 = dx + lc * (dy - dx)
    r2 = dy + lc * (dx - dy)
    g1, g2 = r1 ^ (r1 >> 1), r2 ^ (r2 >> 1)
    near = (g2 == 1) | (g2 == 2)
    chunk = jnp.where(near, 1 + (g1 >> 1), g2)
    minor = jnp.where(near, (g2 - 1) * 2 + (g1 & 1), g1)
    return chunk * 8 + lc * 4 + minor


def quantize(val):
    top = jnp.maximum(jnp.max(jnp.abs(val), axis=1, keepdims=True), 1e-30)
    coded = jnp.round(val * (32767.0 / top)).astype(I32).astype(I16)
    return coded, top * (1.0 / 32767.0)


def widen(coded):
    return coded.astype(I32).astype(F32)


def kernel(hidden, head, row_scale_in, live_in, order_in, blp_in, tlen_in, div_in,
           scored, slotn,
           row_scale, live, order, blp, tlen, div,
           slotv, row8, fold, folded, pool, headv, st, sel, xsel, S, CN,
           SP, SM, RM, RP, SP2, SM2, RM2, RP2,
           CP, CM, KM, KP, CP2, CM2, KM2, KP2,
           TL, TA, TB, LS,
           head_sem, own_sem, in_sem, out_sem, z_s, z_r, t_s, t_r,
           r1_s, r1_r, r2_s, r2_r, sib_s, sib_r,
           rs_s, rs_r, rt_s, rt_r, ta_s, ta_r, tb_s, tb_r, ls_s, ls_r):
    q = lax.axis_index("dp")
    v = lax.axis_index("vocab")
    x, y, c = v // 8, (v // 2) % 4, v % 2
    width = hidden.shape[1] // 4
    voc = head.shape[0]
    half_v = voc // 2
    rows_g = div.shape[1]
    slots = blp.shape[0]
    n_pieces = len(PIECES)

    def dev(zz, xx, yy, cc):
        return (zz % 4, (xx % 4) * 8 + (yy % 4) * 2 + (cc % 2))

    zdev = [dev(q + d, x, y, c) for d in range(4)]
    fan = [(dy, dc) for dy in range(4) for dc in range(2)]
    adev = [dev(q, x, y + dy, c + dc) for dy, dc in fan]
    bdev = [dev(q, x + d, y, c) for d in range(4)]
    sibling = adev[1]
    r1p = dev(q, x + (1 - c), y + c, c)
    r1m = dev(q, x + 3 * (1 - c), y + 3 * c, c)
    r2p = dev(q, x + c, y + (1 - c), c)
    r2m = dev(q, x + 3 * c, y + 3 * (1 - c), c)
    sends = []

    def rc(src, dst, ss, rs, device):
        return pltpu.make_async_remote_copy(
            src_ref=src, dst_ref=dst, send_sem=ss, recv_sem=rs, device_id=device, device_id_type=MESH)

    def push(src, dst, ss, rs, device):
        copy = rc(src, dst, ss, rs, device)
        copy.start()
        sends.append(copy)

    def got(dst, rs):
        rc(dst, dst, t_s.at[0], rs, zdev[1]).wait_recv()

    barrier = pltpu.get_barrier_semaphore()
    peers = zdev[1:] + adev[1:] + bdev[1:]
    for device in peers:
        pl.semaphore_signal(barrier, inc=1, device_id=device, device_id_type=MESH)

    own_copy = pltpu.make_async_copy(hidden, slotv, own_sem)
    own_copy.start()
    small = [pltpu.make_async_copy(src, dst, in_sem.at[i]) for i, (src, dst) in enumerate((
        (blp_in, blp), (tlen_in, tlen), (live_in, live), (order_in, order), (div_in, div), (row_scale_in, row_scale)))]
    for copy in small:
        copy.start()
    head_copy = pltpu.make_async_copy(head, headv, head_sem)
    head_copy.start()
    for copy in small:
        copy.wait()
    st[q] = jnp.zeros(st.shape[1:], F32)
    st[q, 0:1, 0:slots] = blp[...].reshape(1, slots)
    lengths = tlen[...].reshape(1, slots).astype(F32)
    st[q, 1:2, 0:slots] = jnp.exp(0.8 * jnp.log((5.0 + lengths) / 6.0))
    for ref in (CP, CM, CP2, CM2):
        ref[...] = jnp.zeros(ref.shape, F32)
    TL[...] = jnp.zeros(TL.shape, F32)
    TA[0] = jnp.zeros(TA.shape[1:], F32)
    TB[0] = jnp.zeros(TB.shape[1:], F32)
    LS[q] = jnp.zeros(LS.shape[1:], F32)

    own_copy.wait()
    run, hw = width // 16, width // 2
    for g in range(4):
        nine = slotv[:, g * width:(g + 1) * width].astype(F32)
        fold[g * 16:(g + 1) * 16, 0:hw] = jnp.concatenate([nine[0:8, 0:hw], nine[0:8, hw:width]], axis=0).astype(BF16)
        for i in range(16):
            row8[i:i + 1, :] = nine[8:9, i * run:(i + 1) * run]
        fold[g * 16:(g + 1) * 16, hw:hw + run] = row8[...].astype(BF16)

    def rows16(ref, group):
        return ref.at[pl.ds(pl.multiple_of(group * 16, 16), 16), :]

    keep = pltpu.make_async_copy(rows16(fold, q), rows16(folded, q), own_sem)
    keep.start()

    pl.semaphore_wait(barrier, len(peers))

    for d in (2, 1, 3):
        push(rows16(fold, (q + d) % 4), rows16(folded, q), z_s.at[d - 1], z_r.at[d - 1], zdev[d])
    for d in (1, 2, 3):
        push(st.at[q], st.at[q], t_s.at[d - 1], t_r.at[d - 1], zdev[d])

    numbers = order[...].reshape(1, 4 * rows_g)
    by_group = [numbers[:, g * rows_g:(g + 1) * rows_g] for g in range(4)]

    def order_of(group):
        return sum(jnp.where(group == g, by_group[g], 0) for g in range(4))

    for gi, group in enumerate(((q + 2) % 4, (q + 1) % 4, (q + 3) % 4, q)):
        _, lane, _, row = row_info(order_of(group), live)
        at = to_col(place(lane, x, y) * CAP + row, rows_g)
        for b in range(32 * CAP // 128):
            hit = at == iota((rows_g, 128), 1) + 128 * b
            sel[gi * rows_g:(gi + 1) * rows_g, b * 128:(b + 1) * 128] = jnp.where(hit, 1.0, 0.0).astype(BF16)

    base = v * voc

    @pl.loop(0, rows_g // 32)
    def _(b):
        rows = pl.multiple_of(b * 32, 32)
        ids = [to_col(div[j:j + 1, :], 32, rows) - base for j in range(16)]
        for k in range(voc // 256):
            token = iota((32, 256), 1) + k * 256
            acc = jnp.zeros((32, 256), F32)
            for j in range(16):
                acc = acc - jnp.where(ids[j] == token, 0.5, 0.0)
            CN[pl.ds(rows, 32), k * 256:(k + 1) * 256] = acc

    counts = [live_of_lane(live[r], v) for r in range(4)]
    firsts = [0]
    for r in range(3):
        firsts.append(firsts[-1] + counts[r])

    def by_replica(values, r):
        return sum(jnp.where(r == i, values[i], 0) for i in range(4))

    i, j = iota((2 * CAP, 64), 0), iota((2 * CAP, 64), 1)
    replica, depth = j >> 4, j & 7
    hit = ((i >> 5) == ((j >> 3) & 1)) & ((i & 31) == by_replica(firsts, replica) + depth)
    pick = jnp.where(hit & (depth < by_replica(counts, replica)), 1.0, 0.0).astype(BF16)
    i, j = iota((16 * CAP, 64), 0), iota((16 * CAP, 64), 1)
    replica = j >> 4
    hit = ((i >> 5) == (j & 15)) & ((i & 31) == by_replica(firsts, replica) + 8)
    pick8 = jnp.where(hit & (by_replica(counts, replica) > 8), 1.0, 0.0).astype(BF16)

    t4 = 4 * c
    u4 = 4 - t4

    def blk(idx):
        return pool.at[pl.ds(pl.multiple_of(idx * CAP, CAP), CAP), :]

    def half(idx, h):
        return pool.at[pl.ds(pl.multiple_of(idx * CAP + h * (CAP // 2), CAP // 2), CAP // 2), :]

    def to_sibling(ch, m):
        push(blk(ch * 8 + t4 + m), blk(ch * 8 + t4 + m), sib_s.at[ch * 4 + m], sib_r.at[ch * 4 + m], sibling)

    def from_sibling(ch):
        for m in range(4):
            got(blk(ch * 8 + u4 + m), sib_r.at[ch * 4 + m])

    def spread(m):
        ch, mm = 1 + (m >> 1), m & 1
        push(blk(t4 + m), blk(ch * 8 + t4 + 2 + mm), r2_s.at[2 * m + 1], r2_r.at[2 * m + 1], r2p)
        push(blk(t4 + m), blk(ch * 8 + t4 + mm), r2_s.at[2 * m], r2_r.at[2 * m], r2m)

    keep.wait()
    for d in (1, 3, 2):
        got(rows16(folded, (q + 4 - d) % 4), z_r.at[d - 1])
    ninth = jnp.dot(pick8, folded[:, hw:hw + run], preferred_element_type=F32)
    for k in range(0, hw, 1024):
        both = jnp.dot(pick, folded[:, k:k + 1024], preferred_element_type=F32)
        for h in range(2):
            for n in range(0, 1024, run):
                at = h * hw + k + n
                b = at // run
                block = both[h * CAP:(h + 1) * CAP, n:n + run] + ninth[b * CAP:(b + 1) * CAP, :]
                pool[pl.ds(pl.multiple_of(t4 * CAP, CAP), CAP), at:at + run] = block.astype(BF16)

    push(blk(t4), blk(t4 + 2), r1_s.at[1], r1_r.at[1], r1p)
    push(blk(t4), blk(t4 + 1), r1_s.at[0], r1_r.at[0], r1m)
    to_sibling(0, 0)
    spread(0)
    got(blk(t4 + 1), r1_r.at[0])
    push(half(t4 + 1, 0), half(t4 + 3, 0), r1_s.at[2], r1_r.at[2], r1m)
    got(blk(t4 + 2), r1_r.at[1])
    push(half(t4 + 2, 1), half(t4 + 3, 1), r1_s.at[3], r1_r.at[3], r1p)
    spread(1)
    spread(2)
    to_sibling(0, 1)
    to_sibling(0, 2)
    got(half(t4 + 3, 0), r1_r.at[2])
    got(half(t4 + 3, 1), r1_r.at[3])
    spread(3)
    to_sibling(0, 3)

    def relay(m):
        ch, mm = 1 + (m >> 1), m & 1
        got(blk(ch * 8 + t4 + mm), r2_r.at[2 * m])
        push(half(ch * 8 + t4 + mm, 0), half(24 + t4 + m, 0), r2_s.at[8 + 2 * m], r2_r.at[8 + 2 * m], r2m)
        got(blk(ch * 8 + t4 + 2 + mm), r2_r.at[2 * m + 1])
        push(half(ch * 8 + t4 + 2 + mm, 1), half(24 + t4 + m, 1), r2_s.at[9 + 2 * m], r2_r.at[9 + 2 * m], r2p)
        to_sibling(ch, mm)
        to_sibling(ch, 2 + mm)

    def relay_far(first):
        for m in (first, first + 1):
            got(half(24 + t4 + m, 0), r2_r.at[8 + 2 * m])
            got(half(24 + t4 + m, 1), r2_r.at[9 + 2 * m])
            to_sibling(3, m)

    def select(lo, hi, top, end):
        @pl.loop(0, width // 512)
        def _(n):
            cols = pl.ds(pl.multiple_of(n * 512, 512), 512)
            found = jnp.dot(sel[top:end, lo * 256:hi * 256], pool[lo * 256:hi * 256, cols], preferred_element_type=F32)
            xsel[top:end, cols] = (found if lo == 0 else xsel[top:end, cols].astype(F32) + found).astype(BF16)

    def multiply(start, size, lo, hi):
        @pl.loop(start // 256, (start + size) // 256)
        def _(n):
            cols = pl.ds(pl.multiple_of(n * 256, 256), 256)
            S[lo:hi, cols] = lax.dot_general(xsel[lo:hi, :], headv[cols, :], (((1,), (1,)), ((), ())),
                                             preferred_element_type=F32)

    def blocks(body):
        @pl.loop(0, rows_g // RB)
        def _(b):
            body(pl.multiple_of(b * RB, RB))

    def mine(gi, rows):
        return pl.ds(pl.multiple_of(gi * rows_g + rows, 32), RB)

    def piece(p):
        start, size = PIECES[p % n_pieces]
        return start + (p // n_pieces) * half_v, size

    def cols_of(p):
        start, size = piece(p)
        return slice(start, start + size)

    def send_first(p):
        plus, minus = (0, 2) if p < n_pieces else (1, 0)

        def body(rows):
            r = pl.ds(rows, RB)
            for buf, scales, gi in ((SP, CP, plus), (SM, CM, minus)):
                coded, scale = quantize(S[mine(gi, rows), cols_of(p)])
                buf[r, cols_of(p)] = coded
                scales[p] += to_row(scale, 256, rows)

        blocks(body)
        push(SP.at[:, cols_of(p)], RM.at[:, cols_of(p)], rs_s.at[p, 0], rs_r.at[p, 0], zdev[1])
        push(SM.at[:, cols_of(p)], RP.at[:, cols_of(p)], rs_s.at[p, 1], rs_r.at[p, 1], zdev[3])
        push(CP.at[p], KM.at[p], rs_s.at[p, 2], rs_r.at[p, 2], zdev[1])
        push(CM.at[p], KP.at[p], rs_s.at[p, 3], rs_r.at[p, 3], zdev[3])

    def send_second(j):
        for p in (j, j + n_pieces):
            got(RM.at[:, cols_of(p)], rs_r.at[p, 0])
            got(RP.at[:, cols_of(p)], rs_r.at[p, 1])
            got(KM.at[p], rs_r.at[p, 2])
            got(KP.at[p], rs_r.at[p, 3])

        def body(rows):
            r = pl.ds(rows, RB)
            for buf, scales, recv, rscale, gi, p in ((SP2, CP2, RM, KM, 1, j), (SM2, CM2, RP, KP, 2, j + n_pieces)):
                old = widen(recv[r, cols_of(p)]) * to_col(rscale[p], RB, rows)
                coded, scale = quantize(S[mine(gi, rows), cols_of(p)] + old)
                buf[r, cols_of(j)] = coded
                scales[j] += to_row(scale, 256, rows)

        blocks(body)
        push(SP2.at[:, cols_of(j)], RM2.at[:, cols_of(j)], rt_s.at[j, 0], rt_r.at[j, 0], zdev[1])
        push(SM2.at[:, cols_of(j)], RP2.at[:, cols_of(j)], rt_s.at[j, 1], rt_r.at[j, 1], zdev[3])
        push(CP2.at[j], KM2.at[j], rt_s.at[j, 2], rt_r.at[j, 2], zdev[1])
        push(CM2.at[j], KP2.at[j], rt_s.at[j, 3], rt_r.at[j, 3], zdev[3])

    def finish(j):
        got(RM2.at[:, cols_of(j)], rt_r.at[j, 0])
        got(RP2.at[:, cols_of(j)], rt_r.at[j, 1])
        got(KM2.at[j], rt_r.at[j, 2])
        got(KP2.at[j], rt_r.at[j, 3])

        def body(rows):
            r = pl.ds(rows, RB)
            for p, near, nscale, far, fscale in ((j, RP, KP, RM2, KM2), (j + n_pieces, RM, KM, RP2, KP2)):
                total = S[mine(3, rows), cols_of(p)]
                total += widen(near[r, cols_of(p)]) * to_col(nscale[p], RB, rows)
                total += widen(far[r, cols_of(j)]) * to_col(fscale[j], RB, rows)
                logits = total * row_scale[:, cols_of(p)]
                S[mine(3, rows), cols_of(p)] = logits
                top = jnp.max(logits, axis=1, keepdims=True)
                TL[p:p + 1, :] += to_row(top, 256, rows)
                TL[p + 8:p + 9, :] += to_row(jnp.sum(jnp.exp(logits - top), axis=1, keepdims=True), 256, rows)

        blocks(body)

    others, every = 3 * rows_g, 4 * rows_g
    relay(0)
    from_sibling(0)
    relay(1)
    relay(2)
    from_sibling(1)
    select(0, 2, 0, others)
    relay(3)
    relay_far(0)
    from_sibling(2)
    select(2, 3, 0, others)
    relay_far(2)
    from_sibling(3)
    select(3, 4, 0, others)
    head_copy.wait()

    for j in range(n_pieces):
        for p in (j, j + n_pieces):
            multiply(*piece(p), 0, others)
            send_first(p)
        if j >= 1:
            send_second(j - 1)
    select(0, 4, others, every)
    multiply(0, half_v, others, every)
    send_second(n_pieces - 1)
    multiply(half_v, half_v, others, every)

    for d in (1, 2, 3):
        got(st.at[(q + 4 - d) % 4], t_r.at[d - 1])
    replica, lane, depth, _ = row_info(order_of(q), live)
    slot_col = to_col(replica * slots + lane * 9 + depth, rows_g)
    score = jnp.zeros((rows_g, 1), F32)
    factor = jnp.zeros((rows_g, 1), F32)
    for r in range(4):
        hit = slot_col - r * slots == iota((rows_g, st.shape[2]), 1)
        score += jnp.sum(jnp.where(hit, st[r, 0:1, :], 0.0), axis=1, keepdims=True)
        factor += jnp.sum(jnp.where(hit, st[r, 1:2, :], 0.0), axis=1, keepdims=True)
    inverse = 1.0 / factor

    for j in range(n_pieces):
        finish(j)

    def combine(tops, totals):
        top = functools.reduce(jnp.maximum, tops)
        return top, sum(total * jnp.exp(t - top) for t, total in zip(tops, totals))

    top, total = combine([TL[p:p + 1, :] for p in range(2 * n_pieces)], [TL[p + 8:p + 9, :] for p in range(2 * n_pieces)])
    TA[0, 0:1, :] = top
    TA[0, 1:2, :] = total
    for i in range(1, 8):
        push(TA.at[0], TA.at[i], ta_s.at[i], ta_r.at[i], adev[i])
    for i in range(1, 8):
        got(TA.at[i], ta_r.at[i])
    top, total = combine([TA[i, 0:1, :] for i in range(8)], [TA[i, 1:2, :] for i in range(8)])
    TB[0, 0:1, :] = top
    TB[0, 1:2, :] = total
    for i in range(1, 4):
        push(TB.at[0], TB.at[i], tb_s.at[i], tb_r.at[i], bdev[i])
    for i in range(1, 4):
        got(TB.at[i], tb_r.at[i])
    top, total = combine([TB[i, 0:1, :] for i in range(4)], [TB[i, 1:2, :] for i in range(4)])
    lse = to_col(top + jnp.log(total), rows_g)
    LS[q, 0:1, :] = to_row(lse, 256)
    for d in (1, 2, 3):
        push(LS.at[q], LS.at[q], ls_s.at[d - 1], ls_r.at[d - 1], zdev[d])
    shift = score - lse
    outs = []
    for p in range(2 * n_pieces):
        CN[:, cols_of(p)] = (S[3 * rows_g:4 * rows_g, cols_of(p)] + CN[:, cols_of(p)] + shift) * inverse
        copy = pltpu.make_async_copy(CN.at[:, cols_of(p)], scored.at[:, cols_of(p)], out_sem.at[p])
        copy.start()
        outs.append(copy)

    for d in (1, 2, 3):
        got(LS.at[(q + 4 - d) % 4], ls_r.at[d - 1])
    acc = jnp.zeros((1, st.shape[2]), F32)
    for g in range(4):
        replica, lane, depth, _ = row_info(by_group[g], live)
        slot_col = to_col(replica * slots + lane * 9 + depth, rows_g)
        hit = slot_col - q * slots == iota((rows_g, st.shape[2]), 1)
        acc += jnp.sum(jnp.where(hit, to_col(LS[g, 0:1, :], rows_g), 0.0), axis=0, keepdims=True)
    slotn[...] = acc[:, 0:slots].reshape(slots)

    for copy in outs:
        copy.wait()
    for copy in sends:
        copy.wait_send()


def call(hidden, head, row_scale, live, order, blp, tlen, div):
    rows_g, voc, width, slots = div.shape[1], head.shape[0], head.shape[1], blp.shape[0]
    half_v = voc // 2
    n = 2 * len(PIECES)
    dma = pltpu.SemaphoreType.DMA
    vmem = pl.BlockSpec(memory_space=pltpu.VMEM)
    anyspace = pl.BlockSpec(memory_space=pl.ANY)
    hbm = pl.BlockSpec(memory_space=pltpu.HBM)
    return pl.pallas_call(
        kernel,
        out_shape=(jax.ShapeDtypeStruct((rows_g, voc), F32), jax.ShapeDtypeStruct((slots,), F32)),
        in_specs=[hbm] * 8,
        out_specs=(anyspace, vmem),
        scratch_shapes=[
            pltpu.VMEM(row_scale.shape, F32),
            pltpu.SMEM(live.shape, I32),
            pltpu.VMEM(order.shape, I32),
            pltpu.VMEM(blp.shape, F32),
            pltpu.VMEM(tlen.shape, I32),
            pltpu.VMEM(div.shape, I32),
            pltpu.VMEM(hidden.shape, BF16),
            pltpu.VMEM((16, width // 16), F32),
            pltpu.VMEM((64, width // 2 + width // 16), BF16),
            pltpu.VMEM((64, width // 2 + width // 16), BF16),
            pltpu.VMEM((32 * CAP, width), BF16),
            pltpu.VMEM((voc, width), BF16),
            pltpu.VMEM((4, 8, 384), F32),
            pltpu.VMEM((4 * rows_g, 32 * CAP), BF16),
            pltpu.VMEM((4 * rows_g, width), BF16),
            pltpu.VMEM((4 * rows_g, voc), F32),
            pltpu.VMEM((rows_g, voc), F32),
            *[pltpu.VMEM((rows_g, voc), I16)] * 4,
            *[pltpu.VMEM((rows_g, half_v), I16)] * 4,
            *[pltpu.VMEM((n, 1, 256), F32)] * 4,
            *[pltpu.VMEM((n // 2, 1, 256), F32)] * 4,
            pltpu.VMEM((16, 256), F32),
            pltpu.VMEM((8, 8, 256), F32),
            pltpu.VMEM((4, 8, 256), F32),
            pltpu.VMEM((4, 8, 256), F32),
            dma, dma, dma((6,)), dma((n,)),
            dma((3,)), dma((3,)), dma((3,)), dma((3,)),
            dma((4,)), dma((4,)), dma((16,)), dma((16,)), dma((16,)), dma((16,)),
            dma((n, 4)), dma((n, 4)), dma((n // 2, 4)), dma((n // 2, 4)),
            dma((8,)), dma((8,)), dma((4,)), dma((4,)), dma((3,)), dma((3,)),
        ],
        compiler_params=pltpu.CompilerParams(
            collective_id=0, has_side_effects=True, vmem_limit_bytes=60 * 1024 * 1024),
    )(hidden, head, row_scale, live, order, blp, tlen, div)


def per_device(hidden, head, row_scale, live, order, beam_log_prob, token_length, div_ids):
    return call(hidden, head, row_scale[None, :], live, order, beam_log_prob, token_length, div_ids.T)


def solution(mesh):
    return jax.shard_map(
        per_device,
        mesh=mesh,
        in_specs=(
            P(("dp", "vocab"), None),
            P("vocab", "dp"),
            P("vocab"),
            P(),
            P(),
            P("dp"),
            P("dp"),
            P("dp", None),
        ),
        out_specs=(P("dp", "vocab"), P("dp")),
        check_vma=False,
    )
```

```python
import functools

import jax
import jax.numpy as jnp
from jax import lax
from jax.experimental import pallas as pl
from jax.experimental.pallas import tpu as pltpu
from jax.sharding import PartitionSpec as P

F32, BF16, I32, I16 = jnp.float32, jnp.bfloat16, jnp.int32, jnp.int16
MESH = pl.DeviceIdType.MESH

CAP = 32
RB = 192
PIECES = ((0, 256), (256, 512), (768, 256))


def iota(shape, axis):
    return lax.broadcasted_iota(I32, shape, axis)


def to_col(row, n, shift=0):
    width = row.shape[1]
    hit = iota((n, width), 0) + shift == iota((n, width), 1)
    return jnp.sum(jnp.where(hit, row, jnp.zeros_like(row)), axis=1, keepdims=True)


def to_row(col, width, shift=0):
    n = col.shape[0]
    hit = iota((n, width), 0) + shift == iota((n, width), 1)
    return jnp.sum(jnp.where(hit, col, jnp.zeros_like(col)), axis=0, keepdims=True)


def live_of_lane(count, lane):
    return (count - lane + 31) >> 5


def row_info(order, live):
    e0 = live[0]
    e1 = e0 + live[1]
    e2 = e1 + live[2]
    past = [(order >= e).astype(I32) for e in (e0, e1, e2)]
    replica = past[0] + past[1] + past[2]
    within = order - (past[0] * live[0] + past[1] * live[1] + past[2] * live[2])
    lane, depth = within & 31, within >> 5
    row = depth
    for i in range(3):
        row = row + past[i] * live_of_lane(live[i], lane)
    return replica, lane, depth, row


def place(lane, x, y):
    lx, ly, lc = lane >> 3, (lane >> 1) & 3, lane & 1
    dx, dy = (lx - x) & 3, (ly - y) & 3
    r1 = dx + lc * (dy - dx)
    r2 = dy + lc * (dx - dy)
    g1, g2 = r1 ^ (r1 >> 1), r2 ^ (r2 >> 1)
    near = (g2 == 1) | (g2 == 2)
    chunk = jnp.where(near, 1 + (g1 >> 1), g2)
    minor = jnp.where(near, (g2 - 1) * 2 + (g1 & 1), g1)
    return chunk * 8 + lc * 4 + minor


def quantize(val):
    top = jnp.maximum(jnp.max(jnp.abs(val), axis=1, keepdims=True), 1e-30)
    coded = jnp.round(val * (32767.0 / top)).astype(I32).astype(I16)
    return coded, top * (1.0 / 32767.0)


def widen(coded):
    return coded.astype(I32).astype(F32)


def kernel(hidden, head, row_scale_in, live_in, order_in, blp_in, tlen_in, div_in,
           scored, slotn,
           row_scale, live, order, blp, tlen, div,
           slotv, row8, fold, folded, pool, headv, st, sel, xsel, S, CN,
           SP, SM, RM, RP, SP2, SM2, RM2, RP2,
           CP, CM, KM, KP, CP2, CM2, KM2, KP2,
           TL, TA, TB, LS,
           head_sem, own_sem, in_sem, out_sem, z_s, z_r, t_s, t_r,
           r1_s, r1_r, r2_s, r2_r, sib_s, sib_r,
           rs_s, rs_r, rt_s, rt_r, ta_s, ta_r, tb_s, tb_r, ls_s, ls_r):
    q = lax.axis_index("dp")
    v = lax.axis_index("vocab")
    x, y, c = v // 8, (v // 2) % 4, v % 2
    width = hidden.shape[1] // 4
    voc = head.shape[0]
    half_v = voc // 2
    rows_g = div.shape[1]
    slots = blp.shape[0]
    n_pieces = len(PIECES)

    def dev(zz, xx, yy, cc):
        return (zz % 4, (xx % 4) * 8 + (yy % 4) * 2 + (cc % 2))

    zdev = [dev(q + d, x, y, c) for d in range(4)]
    fan = [(dy, dc) for dy in range(4) for dc in range(2)]
    adev = [dev(q, x, y + dy, c + dc) for dy, dc in fan]
    bdev = [dev(q, x + d, y, c) for d in range(4)]
    sibling = adev[1]
    r1p = dev(q, x + (1 - c), y + c, c)
    r1m = dev(q, x + 3 * (1 - c), y + 3 * c, c)
    r2p = dev(q, x + c, y + (1 - c), c)
    r2m = dev(q, x + 3 * c, y + 3 * (1 - c), c)
    sends = []

    def rc(src, dst, ss, rs, device):
        return pltpu.make_async_remote_copy(
            src_ref=src, dst_ref=dst, send_sem=ss, recv_sem=rs, device_id=device, device_id_type=MESH)

    def push(src, dst, ss, rs, device):
        copy = rc(src, dst, ss, rs, device)
        copy.start()
        sends.append(copy)

    def got(dst, rs):
        rc(dst, dst, t_s.at[0], rs, zdev[1]).wait_recv()

    barrier = pltpu.get_barrier_semaphore()
    peers = [zdev[2], bdev[2], adev[5], adev[4], zdev[1], zdev[3], bdev[1], bdev[3]] + adev[1:4] + adev[6:]
    for device in peers:
        pl.semaphore_signal(barrier, inc=1, device_id=device, device_id_type=MESH)

    own_copy = pltpu.make_async_copy(hidden, slotv, own_sem)
    own_copy.start()
    small = [pltpu.make_async_copy(src, dst, in_sem.at[i]) for i, (src, dst) in enumerate((
        (blp_in, blp), (tlen_in, tlen), (live_in, live), (order_in, order), (div_in, div), (row_scale_in, row_scale)))]
    for copy in small:
        copy.start()
    head_copy = pltpu.make_async_copy(head, headv, head_sem)
    head_copy.start()
    for copy in small:
        copy.wait()
    st[q] = jnp.zeros(st.shape[1:], F32)
    st[q, 0:1, 0:slots] = blp[...].reshape(1, slots)
    lengths = tlen[...].reshape(1, slots).astype(F32)
    st[q, 1:2, 0:slots] = jnp.exp(0.8 * jnp.log((5.0 + lengths) / 6.0))
    for ref in (CP, CM, CP2, CM2):
        ref[...] = jnp.zeros(ref.shape, F32)
    TL[...] = jnp.zeros(TL.shape, F32)
    TA[0] = jnp.zeros(TA.shape[1:], F32)
    TB[0] = jnp.zeros(TB.shape[1:], F32)
    LS[q] = jnp.zeros(LS.shape[1:], F32)

    own_copy.wait()
    run, hw = width // 16, width // 2
    for g in range(4):
        nine = slotv[:, g * width:(g + 1) * width].astype(F32)
        fold[g * 16:(g + 1) * 16, 0:hw] = jnp.concatenate([nine[0:8, 0:hw], nine[0:8, hw:width]], axis=0).astype(BF16)
        for i in range(16):
            row8[i:i + 1, :] = nine[8:9, i * run:(i + 1) * run]
        fold[g * 16:(g + 1) * 16, hw:hw + run] = row8[...].astype(BF16)

    def rows16(ref, group):
        return ref.at[pl.ds(pl.multiple_of(group * 16, 16), 16), :]

    keep = pltpu.make_async_copy(rows16(fold, q), rows16(folded, q), own_sem)
    keep.start()

    pl.semaphore_wait(barrier, len(peers))

    for d in (2, 1, 3):
        push(rows16(fold, (q + d) % 4), rows16(folded, q), z_s.at[d - 1], z_r.at[d - 1], zdev[d])
    for d in (1, 2, 3):
        push(st.at[q], st.at[q], t_s.at[d - 1], t_r.at[d - 1], zdev[d])

    numbers = order[...].reshape(1, 4 * rows_g)
    by_group = [numbers[:, g * rows_g:(g + 1) * rows_g] for g in range(4)]

    def order_of(group):
        return sum(jnp.where(group == g, by_group[g], 0) for g in range(4))

    for gi, group in enumerate(((q + 2) % 4, (q + 1) % 4, (q + 3) % 4, q)):
        _, lane, _, row = row_info(order_of(group), live)
        at = to_col(place(lane, x, y) * CAP + row, rows_g)
        for b in range(32 * CAP // 128):
            hit = at == iota((rows_g, 128), 1) + 128 * b
            sel[gi * rows_g:(gi + 1) * rows_g, b * 128:(b + 1) * 128] = jnp.where(hit, 1.0, 0.0).astype(BF16)

    base = v * voc

    @pl.loop(0, rows_g // 32)
    def _(b):
        rows = pl.multiple_of(b * 32, 32)
        ids = [to_col(div[j:j + 1, :], 32, rows) - base for j in range(16)]
        for k in range(voc // 256):
            token = iota((32, 256), 1) + k * 256
            acc = jnp.zeros((32, 256), F32)
            for j in range(16):
                acc = acc - jnp.where(ids[j] == token, 0.5, 0.0)
            CN[pl.ds(rows, 32), k * 256:(k + 1) * 256] = acc

    counts = [live_of_lane(live[r], v) for r in range(4)]
    firsts = [0]
    for r in range(3):
        firsts.append(firsts[-1] + counts[r])

    def by_replica(values, r):
        return sum(jnp.where(r == i, values[i], 0) for i in range(4))

    i, j = iota((2 * CAP, 64), 0), iota((2 * CAP, 64), 1)
    replica, depth = j >> 4, j & 7
    hit = ((i >> 5) == ((j >> 3) & 1)) & ((i & 31) == by_replica(firsts, replica) + depth)
    pick = jnp.where(hit & (depth < by_replica(counts, replica)), 1.0, 0.0).astype(BF16)
    i, j = iota((16 * CAP, 64), 0), iota((16 * CAP, 64), 1)
    replica = j >> 4
    hit = ((i >> 5) == (j & 15)) & ((i & 31) == by_replica(firsts, replica) + 8)
    pick8 = jnp.where(hit & (by_replica(counts, replica) > 8), 1.0, 0.0).astype(BF16)

    t4 = 4 * c
    u4 = 4 - t4

    def blk(idx):
        return pool.at[pl.ds(pl.multiple_of(idx * CAP, CAP), CAP), :]

    def half(idx, h):
        return pool.at[pl.ds(pl.multiple_of(idx * CAP + h * (CAP // 2), CAP // 2), CAP // 2), :]

    def to_sibling(ch, m):
        push(blk(ch * 8 + t4 + m), blk(ch * 8 + t4 + m), sib_s.at[ch * 4 + m], sib_r.at[ch * 4 + m], sibling)

    def from_sibling(ch):
        for m in range(4):
            got(blk(ch * 8 + u4 + m), sib_r.at[ch * 4 + m])

    def spread(m):
        ch, mm = 1 + (m >> 1), m & 1
        push(blk(t4 + m), blk(ch * 8 + t4 + 2 + mm), r2_s.at[2 * m + 1], r2_r.at[2 * m + 1], r2p)
        push(blk(t4 + m), blk(ch * 8 + t4 + mm), r2_s.at[2 * m], r2_r.at[2 * m], r2m)

    keep.wait()
    for d in (1, 3, 2):
        got(rows16(folded, (q + 4 - d) % 4), z_r.at[d - 1])
    ninth = jnp.dot(pick8, folded[:, hw:hw + run], preferred_element_type=F32)
    for k in range(0, hw, 1024):
        both = jnp.dot(pick, folded[:, k:k + 1024], preferred_element_type=F32)
        for h in range(2):
            for n in range(0, 1024, run):
                at = h * hw + k + n
                b = at // run
                block = both[h * CAP:(h + 1) * CAP, n:n + run] + ninth[b * CAP:(b + 1) * CAP, :]
                pool[pl.ds(pl.multiple_of(t4 * CAP, CAP), CAP), at:at + run] = block.astype(BF16)

    push(blk(t4), blk(t4 + 2), r1_s.at[1], r1_r.at[1], r1p)
    push(blk(t4), blk(t4 + 1), r1_s.at[0], r1_r.at[0], r1m)
    to_sibling(0, 0)
    spread(0)
    got(blk(t4 + 1), r1_r.at[0])
    push(half(t4 + 1, 0), half(t4 + 3, 0), r1_s.at[2], r1_r.at[2], r1m)
    got(blk(t4 + 2), r1_r.at[1])
    push(half(t4 + 2, 1), half(t4 + 3, 1), r1_s.at[3], r1_r.at[3], r1p)
    spread(1)
    spread(2)
    to_sibling(0, 1)
    to_sibling(0, 2)
    got(half(t4 + 3, 0), r1_r.at[2])
    got(half(t4 + 3, 1), r1_r.at[3])
    spread(3)
    to_sibling(0, 3)

    def relay(m):
        ch, mm = 1 + (m >> 1), m & 1
        got(blk(ch * 8 + t4 + mm), r2_r.at[2 * m])
        push(half(ch * 8 + t4 + mm, 0), half(24 + t4 + m, 0), r2_s.at[8 + 2 * m], r2_r.at[8 + 2 * m], r2m)
        got(blk(ch * 8 + t4 + 2 + mm), r2_r.at[2 * m + 1])
        push(half(ch * 8 + t4 + 2 + mm, 1), half(24 + t4 + m, 1), r2_s.at[9 + 2 * m], r2_r.at[9 + 2 * m], r2p)
        to_sibling(ch, mm)
        to_sibling(ch, 2 + mm)

    def relay_far(first):
        for m in (first, first + 1):
            got(half(24 + t4 + m, 0), r2_r.at[8 + 2 * m])
            got(half(24 + t4 + m, 1), r2_r.at[9 + 2 * m])
            to_sibling(3, m)

    def select(lo, hi, top, end):
        @pl.loop(0, width // 512)
        def _(n):
            cols = pl.ds(pl.multiple_of(n * 512, 512), 512)
            found = jnp.dot(sel[top:end, lo * 256:hi * 256], pool[lo * 256:hi * 256, cols], preferred_element_type=F32)
            xsel[top:end, cols] = (found if lo == 0 else xsel[top:end, cols].astype(F32) + found).astype(BF16)

    def multiply(start, size, lo, hi):
        @pl.loop(start // 256, (start + size) // 256)
        def _(n):
            cols = pl.ds(pl.multiple_of(n * 256, 256), 256)
            S[lo:hi, cols] = lax.dot_general(xsel[lo:hi, :], headv[cols, :], (((1,), (1,)), ((), ())),
                                             preferred_element_type=F32)

    def blocks(body):
        @pl.loop(0, rows_g // RB)
        def _(b):
            body(pl.multiple_of(b * RB, RB))

    def mine(gi, rows):
        return pl.ds(pl.multiple_of(gi * rows_g + rows, 32), RB)

    def piece(p):
        start, size = PIECES[p % n_pieces]
        return start + (p // n_pieces) * half_v, size

    def cols_of(p):
        start, size = piece(p)
        return slice(start, start + size)

    def send_first(p):
        plus, minus = (0, 2) if p < n_pieces else (1, 0)

        for buf, scales, gi, to, recv, side, device in (
                (SP, CP, plus, RM, KM, 0, zdev[1]), (SM, CM, minus, RP, KP, 1, zdev[3])):
            def body(rows):
                coded, scale = quantize(S[mine(gi, rows), cols_of(p)])
                buf[pl.ds(rows, RB), cols_of(p)] = coded
                scales[p] += to_row(scale, 256, rows)

            blocks(body)
            push(buf.at[:, cols_of(p)], to.at[:, cols_of(p)], rs_s.at[p, side], rs_r.at[p, side], device)
            push(scales.at[p], recv.at[p], rs_s.at[p, side + 2], rs_r.at[p, side + 2], device)

    def send_second(j):
        for p in (j, j + n_pieces):
            got(RM.at[:, cols_of(p)], rs_r.at[p, 0])
            got(RP.at[:, cols_of(p)], rs_r.at[p, 1])
            got(KM.at[p], rs_r.at[p, 2])
            got(KP.at[p], rs_r.at[p, 3])

        def body(rows):
            r = pl.ds(rows, RB)
            for buf, scales, recv, rscale, gi, p in ((SP2, CP2, RM, KM, 1, j), (SM2, CM2, RP, KP, 2, j + n_pieces)):
                old = widen(recv[r, cols_of(p)]) * to_col(rscale[p], RB, rows)
                coded, scale = quantize(S[mine(gi, rows), cols_of(p)] + old)
                buf[r, cols_of(j)] = coded
                scales[j] += to_row(scale, 256, rows)

        blocks(body)
        push(SP2.at[:, cols_of(j)], RM2.at[:, cols_of(j)], rt_s.at[j, 0], rt_r.at[j, 0], zdev[1])
        push(SM2.at[:, cols_of(j)], RP2.at[:, cols_of(j)], rt_s.at[j, 1], rt_r.at[j, 1], zdev[3])
        push(CP2.at[j], KM2.at[j], rt_s.at[j, 2], rt_r.at[j, 2], zdev[1])
        push(CM2.at[j], KP2.at[j], rt_s.at[j, 3], rt_r.at[j, 3], zdev[3])

    def finish(j):
        got(RM2.at[:, cols_of(j)], rt_r.at[j, 0])
        got(RP2.at[:, cols_of(j)], rt_r.at[j, 1])
        got(KM2.at[j], rt_r.at[j, 2])
        got(KP2.at[j], rt_r.at[j, 3])

        def body(rows):
            r = pl.ds(rows, RB)
            for p, near, nscale, far, fscale in ((j, RP, KP, RM2, KM2), (j + n_pieces, RM, KM, RP2, KP2)):
                total = S[mine(3, rows), cols_of(p)]
                total += widen(near[r, cols_of(p)]) * to_col(nscale[p], RB, rows)
                total += widen(far[r, cols_of(j)]) * to_col(fscale[j], RB, rows)
                logits = total * row_scale[:, cols_of(p)]
                S[mine(3, rows), cols_of(p)] = logits
                top = jnp.max(logits, axis=1, keepdims=True)
                TL[p:p + 1, :] += to_row(top, 256, rows)
                TL[p + 8:p + 9, :] += to_row(jnp.sum(jnp.exp(logits - top), axis=1, keepdims=True), 256, rows)

        blocks(body)

    others, every = 3 * rows_g, 4 * rows_g
    relay(0)
    from_sibling(0)
    relay(1)
    relay(2)
    from_sibling(1)
    select(0, 2, 0, others)
    relay(3)
    relay_far(0)
    from_sibling(2)
    select(2, 3, 0, others)
    relay_far(2)
    from_sibling(3)
    select(3, 4, 0, others)
    head_copy.wait()

    for j in range(n_pieces):
        for p in (j, j + n_pieces):
            multiply(*piece(p), 0, others)
            send_first(p)
        if j >= 1:
            send_second(j - 1)
    select(0, 4, others, every)
    multiply(0, half_v, others, every)
    send_second(n_pieces - 1)
    multiply(half_v, half_v, others, every)

    for d in (1, 2, 3):
        got(st.at[(q + 4 - d) % 4], t_r.at[d - 1])
    replica, lane, depth, _ = row_info(order_of(q), live)
    slot_col = to_col(replica * slots + lane * 9 + depth, rows_g)
    score = jnp.zeros((rows_g, 1), F32)
    factor = jnp.zeros((rows_g, 1), F32)
    for r in range(4):
        hit = slot_col - r * slots == iota((rows_g, st.shape[2]), 1)
        score += jnp.sum(jnp.where(hit, st[r, 0:1, :], 0.0), axis=1, keepdims=True)
        factor += jnp.sum(jnp.where(hit, st[r, 1:2, :], 0.0), axis=1, keepdims=True)
    inverse = 1.0 / factor

    for j in range(n_pieces):
        finish(j)

    def combine(tops, totals):
        top = functools.reduce(jnp.maximum, tops)
        return top, sum(total * jnp.exp(t - top) for t, total in zip(tops, totals))

    top, total = combine([TL[p:p + 1, :] for p in range(2 * n_pieces)], [TL[p + 8:p + 9, :] for p in range(2 * n_pieces)])
    TA[0, 0:1, :] = top
    TA[0, 1:2, :] = total
    for i in (5, 4, 3, 7, 2, 6, 1):
        push(TA.at[0], TA.at[i], ta_s.at[i], ta_r.at[i], adev[i])
    for i in range(1, 8):
        got(TA.at[i], ta_r.at[i])
    top, total = combine([TA[i, 0:1, :] for i in range(8)], [TA[i, 1:2, :] for i in range(8)])
    TB[0, 0:1, :] = top
    TB[0, 1:2, :] = total
    for i in (2, 1, 3):
        push(TB.at[0], TB.at[i], tb_s.at[i], tb_r.at[i], bdev[i])
    for i in range(1, 4):
        got(TB.at[i], tb_r.at[i])
    top, total = combine([TB[i, 0:1, :] for i in range(4)], [TB[i, 1:2, :] for i in range(4)])
    lse_row = top + jnp.log(total)
    LS[q, 0:1, :] = lse_row
    for d in (2, 1, 3):
        push(LS.at[q], LS.at[q], ls_s.at[d - 1], ls_r.at[d - 1], zdev[d])
    shift = score - to_col(lse_row, rows_g)
    outs = []
    for p in range(2 * n_pieces):
        CN[:, cols_of(p)] = (S[3 * rows_g:4 * rows_g, cols_of(p)] + CN[:, cols_of(p)] + shift) * inverse
        copy = pltpu.make_async_copy(CN.at[:, cols_of(p)], scored.at[:, cols_of(p)], out_sem.at[p])
        copy.start()
        outs.append(copy)

    for d in (1, 2, 3):
        got(LS.at[(q + 4 - d) % 4], ls_r.at[d - 1])
    acc = jnp.zeros((1, st.shape[2]), F32)
    for g in range(4):
        replica, lane, depth, _ = row_info(by_group[g], live)
        slot_col = to_col(replica * slots + lane * 9 + depth, rows_g)
        hit = slot_col - q * slots == iota((rows_g, st.shape[2]), 1)
        acc += jnp.sum(jnp.where(hit, to_col(LS[g, 0:1, :], rows_g), 0.0), axis=0, keepdims=True)
    slotn[...] = acc[:, 0:slots].reshape(slots)

    for copy in outs:
        copy.wait()
    for copy in sends:
        copy.wait_send()


def call(hidden, head, row_scale, live, order, blp, tlen, div):
    rows_g, voc, width, slots = div.shape[1], head.shape[0], head.shape[1], blp.shape[0]
    half_v = voc // 2
    n = 2 * len(PIECES)
    dma = pltpu.SemaphoreType.DMA
    vmem = pl.BlockSpec(memory_space=pltpu.VMEM)
    anyspace = pl.BlockSpec(memory_space=pl.ANY)
    hbm = pl.BlockSpec(memory_space=pltpu.HBM)
    return pl.pallas_call(
        kernel,
        out_shape=(jax.ShapeDtypeStruct((rows_g, voc), F32), jax.ShapeDtypeStruct((slots,), F32)),
        in_specs=[hbm] * 8,
        out_specs=(anyspace, vmem),
        scratch_shapes=[
            pltpu.VMEM(row_scale.shape, F32),
            pltpu.SMEM(live.shape, I32),
            pltpu.VMEM(order.shape, I32),
            pltpu.VMEM(blp.shape, F32),
            pltpu.VMEM(tlen.shape, I32),
            pltpu.VMEM(div.shape, I32),
            pltpu.VMEM(hidden.shape, BF16),
            pltpu.VMEM((16, width // 16), F32),
            pltpu.VMEM((64, width // 2 + width // 16), BF16),
            pltpu.VMEM((64, width // 2 + width // 16), BF16),
            pltpu.VMEM((32 * CAP, width), BF16),
            pltpu.VMEM((voc, width), BF16),
            pltpu.VMEM((4, 8, 384), F32),
            pltpu.VMEM((4 * rows_g, 32 * CAP), BF16),
            pltpu.VMEM((4 * rows_g, width), BF16),
            pltpu.VMEM((4 * rows_g, voc), F32),
            pltpu.VMEM((rows_g, voc), F32),
            *[pltpu.VMEM((rows_g, voc), I16)] * 4,
            *[pltpu.VMEM((rows_g, half_v), I16)] * 4,
            *[pltpu.VMEM((n, 1, 256), F32)] * 4,
            *[pltpu.VMEM((n // 2, 1, 256), F32)] * 4,
            pltpu.VMEM((16, 256), F32),
            pltpu.VMEM((8, 8, 256), F32),
            pltpu.VMEM((4, 8, 256), F32),
            pltpu.VMEM((4, 8, 256), F32),
            dma, dma, dma((6,)), dma((n,)),
            dma((3,)), dma((3,)), dma((3,)), dma((3,)),
            dma((4,)), dma((4,)), dma((16,)), dma((16,)), dma((16,)), dma((16,)),
            dma((n, 4)), dma((n, 4)), dma((n // 2, 4)), dma((n // 2, 4)),
            dma((8,)), dma((8,)), dma((4,)), dma((4,)), dma((3,)), dma((3,)),
        ],
        compiler_params=pltpu.CompilerParams(
            collective_id=0, has_side_effects=True, vmem_limit_bytes=60 * 1024 * 1024),
    )(hidden, head, row_scale, live, order, blp, tlen, div)


def per_device(hidden, head, row_scale, live, order, beam_log_prob, token_length, div_ids):
    return call(hidden, head, row_scale[None, :], live, order, beam_log_prob, token_length, div_ids.T)


def solution(mesh):
    return jax.shard_map(
        per_device,
        mesh=mesh,
        in_specs=(
            P(("dp", "vocab"), None),
            P("vocab", "dp"),
            P("vocab"),
            P(),
            P(),
            P("dp"),
            P("dp"),
            P("dp", None),
        ),
        out_specs=(P("dp", "vocab"), P("dp")),
        check_vma=False,
    )
```
